256 devices in a mesh: row: 32 (over y_lo, z, core), col: 8 (over y_hi, x).
Axes of the slice: x: 4, y: 4 (y_hi: 2, y_lo: 2; y = y_hi * 2 + y_lo), z: 8, core: 2. Of those that a mesh axis runs over, the one named last changes fastest.
Arguments:
- coefficients: float32 [1024, 64], P(('row', 'col')), may hold values from -3 to 3
- off_x: int32 [1024], P(('row', 'col')), may hold values from 0 to 31
- off_y: int32 [1024], P(('row', 'col')), may hold values from 0 to 31
- off_z: int32 [1024], P(('row', 'col')), may hold values from 0 to 127
- external: float32 [1024, 256, 128], P('row', 'col'), may hold values from -6 to 6
- pattern: int32 [128, 128], replicated, may hold values from 0 to 1, as said below
- hamiltonian: bfloat16 [8192, 8192], P('row', 'col'), may hold values from -0.125 to 0.125
- density_matrix: bfloat16 [8192, 8192], P('row', 'col'), may hold values from -6 to 6
Outputs:
- density: float32 [1024, 256, 128], P('row', 'col')
- integrals: float32 [1024, 64], P(('row', 'col'))
- product: float32 [8192, 8192], P('row', 'col')
The draws below stay inside these ranges and needn't reach their ends.
Inputs may be any that keep to these rules, and one draw needn't show every extreme that they name: `pattern`: each tile of 4 x 16 blocks that one device holds (block rows of one index of row, block columns of one index of col) has at most 24 ones, and some tile has exactly 24.
All inputs are finite; a program needn't handle non-finite values.
Results may differ from the reference program's by a relative error of at most 0.00045.
Values may be sent and summed in bfloat16 or wider, within the bound.
No kernel may reach another device: no remote copies, remote signals or barrier semaphores. Data moves between devices by JAX's collectives and lax.ppermute only.
A program may use at most 128 MiB of HBM per device.

```python
import jax
import jax.numpy as jnp
from jax import lax

BS = 64
BASIS = 8
NCOMP = 64
CUBE = 32
GX = 32
GY = 32
GZ = 128
ATOM_DEV = 4
ATOMS = 1024
NX = 1024
NY = 256
ORDER = 8192
NB = 128
RB = 4
CB = 16
TB = 64
PCAP = 24
N_COL = 8


def draw_pattern(key, part):
    row_tiles = NB // RB
    col_tiles = NB // CB
    tile_total = row_tiles * col_tiles
    key_count, key_fullest, key_ranking = jax.random.split(jax.random.fold_in(key, 17), 3)
    lowest = max(PCAP // 2, 1)
    counts = jax.random.randint(key_count, (tile_total,), lowest, PCAP + 1)
    fullest = jax.random.randint(key_fullest, (), 0, tile_total)
    counts = jnp.where(jnp.arange(tile_total) == fullest, PCAP, counts)
    tile_keys = jax.random.split(key_ranking, tile_total)
    ranking = jax.vmap(lambda tile_key: jax.random.permutation(tile_key, TB))(tile_keys)
    chosen = (ranking < counts[:, None]).astype(jnp.int32)
    return chosen.reshape(row_tiles, col_tiles, RB, CB).transpose(0, 2, 1, 3).reshape(NB, NB)


def place_ends(values, stream_key, least, largest):
    spot = [jax.random.randint(jax.random.fold_in(stream_key, axis), (), 0, length) for axis, length in enumerate(values.shape)]
    widest = values.shape.index(max(values.shape))
    neighbour = spot[:widest] + [(spot[widest] + 1) % values.shape[widest]] + spot[widest + 1:]
    return values.at[tuple(spot)].set(least).at[tuple(neighbour)].set(largest)


def steps_of(stream_key, shape, pieces, smallest, largest):
    def one(axis_at, shards_of):
        heights = jax.random.uniform(jax.random.fold_in(jax.random.fold_in(stream_key, 6), axis_at), (shards_of,), jnp.float32, smallest / len(pieces), largest / len(pieces))
        return jnp.repeat(jnp.exp(heights), shape[axis_at] // shards_of).reshape((-1,) + (1,) * (len(shape) - axis_at - 1))

    loudness = one(*pieces[0])
    for cut in pieces[1:]:
        loudness = loudness * one(*cut)
    return loudness


def scatter_about(key, extent, deviation, reach, cuts=(), kind=jnp.bfloat16):
    factor_of = steps_of(key, extent, cuts, -0.22, 0.18) if cuts else 1.0
    values = jax.random.normal(key, extent, jnp.float32) * deviation * factor_of
    return jnp.minimum(jnp.maximum(values, -reach), reach).astype(kind)


def setup_inputs(seed: int = 0) -> dict:
    seeds = jax.random.split(jax.random.key(seed), 9)
    return {
        "coefficients": scatter_about(seeds[0], (ATOMS, NCOMP), 0.5, 3.0, ((0, 256),), jnp.float32),
        "off_x": place_ends(jax.random.randint(seeds[1], (ATOMS,), 0, GX), jax.random.fold_in(seeds[1], 1), 0, GX - 1).astype(jnp.int32),
        "off_y": place_ends(jax.random.randint(seeds[2], (ATOMS,), 0, GY), jax.random.fold_in(seeds[2], 1), 0, GY - 1).astype(jnp.int32),
        "off_z": place_ends(jax.random.randint(seeds[3], (ATOMS,), 0, GZ), jax.random.fold_in(seeds[3], 1), 0, GZ - 1).astype(jnp.int32),
        "external": scatter_about(seeds[4], (NX, NY, GZ), 1.0, 6.0, ((0, 32), (1, 8)), jnp.float32),
        "pattern": draw_pattern(jax.random.fold_in(seeds[8], 71), 0),
        "hamiltonian": scatter_about(seeds[6], (ORDER, ORDER), (ORDER // 4) ** -0.5, 0.125, ((0, 32), (1, 8))),
        "density_matrix": scatter_about(seeds[7], (ORDER, ORDER), 1.0, 6.0, ((0, 32), (1, 8))),
    }


PRECISE = lax.Precision.HIGHEST


def hermite(distance):
    scaled = (distance.astype(jnp.float32) + 0.5 - CUBE / 2.0) * (6.0 / CUBE)
    gaussian = jnp.exp(-0.5 * scaled * scaled)
    return jnp.stack([gaussian, scaled * gaussian, scaled * scaled * gaussian, scaled * scaled * scaled * gaussian], axis=0)


def fold_axis(grid_sum, axis, length):
    half_cube = CUBE // 2
    core_part = lax.slice_in_dim(grid_sum, half_cube, half_cube + length, axis=axis)
    below = lax.slice_in_dim(grid_sum, 0, half_cube, axis=axis)
    above = lax.slice_in_dim(grid_sum, length + half_cube, length + CUBE, axis=axis)
    widths_low = [(0, 0)] * 3
    widths_low[axis] = (length - half_cube, 0)
    widths_high = [(0, 0)] * 3
    widths_high[axis] = (0, length - half_cube)
    return core_part + jnp.pad(below, widths_low) + jnp.pad(above, widths_high)


def reference(coefficients, off_x, off_y, off_z, external, pattern, hamiltonian, density_matrix):
    atom_ids = jnp.arange(ATOMS, dtype=jnp.int32)
    device_ids = atom_ids // ATOM_DEV
    centre_x = ((device_ids // N_COL) * GX + off_x).astype(jnp.int32)
    centre_y = ((device_ids % N_COL) * GY + off_y).astype(jnp.int32)
    centre_z = off_z.astype(jnp.int32)
    basis_table = hermite(jnp.arange(CUBE, dtype=jnp.int32))
    coef_cube = coefficients.reshape(ATOMS, 4, 4, 4)

    def add_cube(atom_index, grid_sum):
        cube_values = jnp.einsum('ijk,ie,jf,kz->efz', coef_cube[atom_index], basis_table, basis_table, basis_table, precision=PRECISE)
        corner = (centre_x[atom_index], centre_y[atom_index], centre_z[atom_index])
        current = lax.dynamic_slice(grid_sum, corner, (CUBE, CUBE, CUBE))
        return lax.dynamic_update_slice(grid_sum, current + cube_values, corner)

    grid_sum = jnp.zeros((NX + CUBE, NY + CUBE, GZ + CUBE), jnp.float32)
    grid_sum = lax.fori_loop(0, ATOMS, add_cube, grid_sum)
    grid_sum = fold_axis(grid_sum, 0, NX)
    grid_sum = fold_axis(grid_sum, 1, NY)
    density = fold_axis(grid_sum, 2, GZ)
    potential = external + jnp.tanh(density)
    wrapped = jnp.pad(potential, CUBE // 2, mode='wrap')
    volume = (6.0 / CUBE) ** 3

    def integrate_atom(atom_index):
        corner = (centre_x[atom_index], centre_y[atom_index], centre_z[atom_index])
        cube_values = lax.dynamic_slice(wrapped, corner, (CUBE, CUBE, CUBE))
        result = jnp.einsum('efz,ie,jf,kz->ijk', cube_values, basis_table, basis_table, basis_table, precision=PRECISE)
        return result.reshape(NCOMP) * volume

    integrals = lax.map(integrate_atom, atom_ids)
    block_mask = jnp.repeat(jnp.repeat(pattern, BS, axis=0), BS, axis=1).astype(jnp.float32)
    h_sparse = hamiltonian.astype(jnp.float32) * block_mask
    p_sparse = density_matrix.astype(jnp.float32) * block_mask
    product = jnp.dot(h_sparse, p_sparse, precision=PRECISE)
    atom_block = integrals.reshape(ATOMS, BASIS, BASIS)
    local_term = jnp.einsum('anm,amj->anj', atom_block, p_sparse.reshape(ATOMS, BASIS, ORDER), precision=PRECISE)
    product = product + local_term.reshape(ORDER, ORDER)
    return density, integrals, product
```

```python
import functools

import jax
import jax.numpy as jnp
from jax import lax
from jax.experimental import pallas as pl
from jax.experimental.pallas import tpu as pltpu
from jax.sharding import PartitionSpec as P

BS = 64
CUBE = 32
SLOTS = 24
PACK = SLOTS // 2 * BS
F32 = jnp.float32
BF16 = jnp.bfloat16
PRECISE = lax.Precision.HIGHEST
SCALE = 6.0 / CUBE


def swap_halves(block):
    return jnp.concatenate([block[:, BS:], block[:, :BS]], axis=1)


def pack_kernel(pattern_ref, h_ref, p_ref, hp_ref, pp_ref, rows, places, sem):
    row, col = lax.axis_index("row"), lax.axis_index("col")
    copy = pltpu.make_async_copy(
        pattern_ref.at[pl.ds(pl.multiple_of(row // 2 * 8, 8), 8), :], rows, sem
    )
    copy.start()
    copy.wait()
    places[SLOTS] = 0

    def clear(i, _):
        places[i] = 0
        return 0

    lax.fori_loop(0, SLOTS, clear, 0)

    def scan(block, count):
        places[count] = block
        flag = rows[row % 2 * 4 + block // 16, col * 16 + block % 16]
        return count + jnp.where(flag != 0, 1, 0)

    lax.fori_loop(0, 64, scan, 0)
    left = lax.broadcasted_iota(jnp.int32, (BS, 2 * BS), 1) < BS
    for source, target in ((p_ref, pp_ref), (h_ref, hp_ref)):
        for pair in range(SLOTS // 2):
            halves = []
            for half in range(2):
                place = places[2 * pair + half]
                r, c = place // 16, place % 16
                block = source[
                    pl.ds(pl.multiple_of(r * BS, BS), BS),
                    pl.ds(pl.multiple_of(c // 2 * 128, 128), 128),
                ]
                halves.append(jnp.where(c % 2 == half, block, swap_halves(block)))
            target[pl.ds(pair * BS, BS), :] = jnp.where(left, halves[0], halves[1])


def pack(pattern, hamiltonian, density_matrix):
    packed = jax.ShapeDtypeStruct((PACK, 128), BF16)
    vmem = pl.BlockSpec(memory_space=pltpu.VMEM)
    return pl.pallas_call(
        pack_kernel,
        out_shape=(packed, packed),
        in_specs=[pl.BlockSpec(memory_space=pl.ANY), vmem, vmem],
        out_specs=(vmem, vmem),
        scratch_shapes=[
            pltpu.SMEM((8, 128), jnp.int32),
            pltpu.SMEM((SLOTS + 8,), jnp.int32),
            pltpu.SemaphoreType.DMA,
        ],
        compiler_params=pltpu.CompilerParams(vmem_limit_bytes=8 * 2**20),
        cost_estimate=pl.CostEstimate(flops=0, bytes_accessed=4 * 2**20, transcendentals=0),
    )(pattern, hamiltonian, density_matrix)


def block_offsets(tiles):
    flags = (tiles != 0).astype(F32)
    earlier = (
        lax.broadcasted_iota(jnp.int32, (64, 64), 0) < lax.broadcasted_iota(jnp.int32, (64, 64), 1)
    ).astype(F32)
    slot = jnp.dot(flags, earlier, precision=PRECISE).astype(jnp.int32)
    parity = lax.broadcasted_iota(jnp.int32, slot.shape, 1) % 2
    at = slot // 2 * BS + jnp.where(slot % 2 == parity, 0, PACK)
    return jnp.where(flags > 0, at, 2 * PACK)


def tile_tables(pattern):
    row, col = lax.axis_index("row"), lax.axis_index("col")
    mine = lax.dynamic_slice(pattern, (0, col * 16), (128, 16)).reshape(32, 64)
    across = lax.dynamic_slice(pattern, (row * 4, 0), (4, 128))
    across = across.reshape(4, 8, 16).transpose(1, 0, 2).reshape(8, 64)
    table = block_offsets(jnp.concatenate([mine, across], axis=0))
    return table[:32], table[32:]


def spread_tile(packed, table_ref, tile, both, store):
    both[0:PACK, :] = packed
    both[PACK : 2 * PACK, :] = swap_halves(packed)
    left = lax.broadcasted_iota(jnp.int32, (BS, 2 * BS), 1) < BS
    for r in range(4):
        for c in range(8):
            at0 = pl.multiple_of(table_ref[tile, r * 16 + 2 * c], BS)
            at1 = pl.multiple_of(table_ref[tile, r * 16 + 2 * c + 1], BS)
            block = jnp.where(left, both[pl.ds(at0, BS), :], both[pl.ds(at1, BS), :])
            store(r, c, block)


def spread_kernel(order, count, table_ref, *refs):
    parts, out_ref, both = refs[:count], refs[count], refs[count + 1]
    col = lax.axis_index("col")
    y, x = col // 4, col % 4
    both[2 * PACK :, :] = jnp.zeros((BS, 128), BF16)
    for part, dx in order:

        def one(j, _, part=part, dx=dx):
            if callable(dx):
                turn = dx(lax.axis_index("row") % 2)
            else:
                turn = dx
            source = (y + j) % 2 * 4 + (x + turn) % 4
            packed = parts[part][pl.ds(pl.multiple_of(j * PACK, PACK), PACK), :]

            def store(r, c, block):
                out_ref[
                    source * 4 + c // 2, r * BS : (r + 1) * BS, c % 2 * 128 : c % 2 * 128 + 128
                ] = block

            spread_tile(packed, table_ref, source, both, store)
            return 0

        lax.fori_loop(0, 2, one, 0)


def spread_hamiltonian(table, parts, order):
    vmem = pl.BlockSpec(memory_space=pltpu.VMEM)
    return pl.pallas_call(
        functools.partial(spread_kernel, order, len(parts)),
        out_shape=jax.ShapeDtypeStruct((32, 256, 256), BF16),
        in_specs=[pl.BlockSpec(memory_space=pltpu.SMEM)] + [vmem] * len(parts),
        out_specs=vmem,
        scratch_shapes=[pltpu.VMEM((2 * PACK + BS, 128), BF16)],
        compiler_params=pltpu.CompilerParams(vmem_limit_bytes=16 * 2**20),
        cost_estimate=pl.CostEstimate(flops=0, bytes_accessed=12 * 2**20, transcendentals=0),
    )(table, *parts)


def split3(value):
    high = value.astype(BF16)
    rest = value - high.astype(F32)
    middle = rest.astype(BF16)
    return high, middle, (rest - middle.astype(F32)).astype(BF16)


def accumulate_kernel(groups, start, local, table_ref, h_ref, *refs):
    refs = list(refs)
    before = None if start else refs.pop(0)
    atoms = refs.pop(0) if local else None
    parts = [refs.pop(0) for _ in groups]
    out_ref, both, dense, wide = refs
    row = lax.axis_index("row")
    y, z, core = row // 16, row // 2 % 8, row % 2
    direction = 1 - 2 * core
    both[2 * PACK :, :] = jnp.zeros((BS, 128), BF16)
    first = True
    for at in range(0, len(groups), 2):
        pair = groups[at : at + 2]
        for g, (steps, flip) in enumerate(pair):
            part = parts[at + g]

            def one(j, _, part=part, steps=steps, flip=flip, g=g):
                tile = ((y + j) % 2 * 8 + (z + steps * direction + 8) % 8) * 2 + (core + flip) % 2
                packed = part[pl.ds(pl.multiple_of(j * PACK, PACK), PACK), :]
                base = pl.multiple_of((2 * g + j) * 256, 256)

                def store(r, c, block):
                    dense[pl.ds(base + r * BS, BS), c * 128 : c * 128 + 128] = block

                spread_tile(packed, table_ref, tile, both, store)
                wide[:, pl.ds(base, 256)] = h_ref[tile]
                return 0

            lax.fori_loop(0, 2, one, 0)
        depth = len(pair) * 512
        if local and at == 0:
            values = atoms[...]
            lane_atom = lax.broadcasted_iota(jnp.int32, (256, 128), 1) // 4
            row_atom = lax.broadcasted_iota(jnp.int32, (256, 128), 0) // 8
            tall = [
                jnp.where(
                    lane_atom == row_atom,
                    jnp.concatenate([values[8 * b : 8 * b + 8, :]] * 32, axis=0),
                    0.0,
                )
                for b in range(2)
            ]
            q = lax.broadcasted_iota(jnp.int32, (256, 256), 0)
            m = lax.broadcasted_iota(jnp.int32, (256, 256), 1)
            place = q % 128 // 4 * 8 + q // 128 * 4 + q % 4
            chosen = jnp.where(place == m, 1.0, 0.0).astype(BF16)
            terms = [
                jnp.dot(t, chosen, preferred_element_type=F32).astype(BF16)
                for t in split3(jnp.concatenate(tall, axis=1))
            ]
        for n in range(4):
            lanes = slice(n * 256, n * 256 + 256)
            total = jnp.dot(
                wide[:, :depth], dense[:depth, lanes], preferred_element_type=F32
            )
            if local and at == 0:
                for term in terms:
                    total += jnp.dot(term, dense[0:256, lanes], preferred_element_type=F32)
            if first:
                if before is not None:
                    total += before[:, lanes]
                out_ref[:, lanes] = total
            else:
                out_ref[:, lanes] += total
        first = False


def accumulate(table, h_dense, before, parts, groups, atoms=None):
    vmem = pl.BlockSpec(memory_space=pltpu.VMEM)
    operands = [table, h_dense]
    if before is not None:
        operands.append(before)
    if atoms is not None:
        operands.append(atoms)
    operands += parts
    depth = 512 * min(2, len(groups))
    return pl.pallas_call(
        functools.partial(accumulate_kernel, groups, before is None, atoms is not None),
        out_shape=jax.ShapeDtypeStruct((256, 1024), F32),
        in_specs=[pl.BlockSpec(memory_space=pltpu.SMEM)] + [vmem] * (len(operands) - 1),
        out_specs=vmem,
        scratch_shapes=[
            pltpu.VMEM((2 * PACK + BS, 128), BF16),
            pltpu.VMEM((depth, 1024), BF16),
            pltpu.VMEM((256, depth), BF16),
        ],
        compiler_params=pltpu.CompilerParams(vmem_limit_bytes=24 * 2**20),
        cost_estimate=pl.CostEstimate(
            flops=2 * 256 * 512 * 1024 * len(groups), bytes_accessed=8 * 2**20, transcendentals=0
        ),
    )(*operands)


def hermite(distance):
    scaled = (distance + (0.5 - CUBE / 2.0)) * SCALE
    inside = (distance >= 0) & (distance < CUBE)
    gaussian = jnp.where(inside, jnp.exp(-0.5 * scaled * scaled), 0.0)
    return gaussian, scaled


def powers(distance):
    gaussian, scaled = hermite(distance)
    first = scaled * gaussian
    second = scaled * first
    return gaussian, first, second, scaled * second


ROWS = [(a, 2 * bh + bl) for bl in range(2) for a in range(4) for bh in range(2)]


def grid_kernel(info_ref, external_ref, density_ref, share_ref, gx_ref, gy_ref, gz_ref, u_ref, s_ref):
    lanes = 256
    cell = lax.broadcasted_iota(jnp.int32, (CUBE, lanes), 0).astype(F32)
    off_x, off_y, off_z = (info_ref[16 + k : 17 + k, :] for k in range(3))
    for n, value in enumerate(powers(cell - off_x + CUBE // 2)):
        gx_ref[n] = value
    for n, value in enumerate(powers(cell - off_y + CUBE // 2)):
        gy_ref[n] = value
    deep = lax.broadcasted_iota(jnp.int32, (128, lanes), 0).astype(F32)
    away = deep - off_z + CUBE // 2
    away = jnp.where(away < 0, away + 128.0, away)
    away = jnp.where(away >= 128, away - 128.0, away)
    kinds = powers(away)
    e = lax.broadcasted_iota(jnp.int32, (128, lanes), 1) % 4
    gz_ref[...] = jnp.where(e == 0, kinds[0], jnp.where(e == 1, kinds[1], jnp.where(e == 2, kinds[2], kinds[3])))
    for b in range(4):
        total = None
        for a in range(4):
            at = ROWS.index((a, b))
            term = info_ref[at : at + 1, :] * gx_ref[a]
            total = term if total is None else total + term
        u_ref[b] = total
    s_ref[...] = jnp.zeros_like(s_ref)
    gz = gz_ref[...]
    chunk = 8

    def step(i, _):
        planes = []
        x0 = pl.multiple_of(i * chunk, chunk)
        rows_u = [u_ref[b, pl.ds(x0, chunk), :] for b in range(4)]
        rows_g = [gx_ref[a, pl.ds(x0, chunk), :] for a in range(4)]
        for x in range(chunk):
            plane = None
            for b in range(4):
                term = rows_u[b][x : x + 1, :] * gy_ref[b]
                plane = term if plane is None else plane + term
            planes.append(plane)
        spread = jnp.concatenate(planes, axis=0)
        density = lax.dot_general(
            spread, gz, (((1,), (1,)), ((), ())), precision=PRECISE, preferred_element_type=F32
        )
        density = density.reshape(chunk, CUBE, 128)
        density_ref[pl.ds(x0, chunk)] = density
        potential = external_ref[pl.ds(x0, chunk)] + jnp.tanh(density)
        along = jnp.dot(
            potential.reshape(chunk * CUBE, 128), gz, precision=PRECISE, preferred_element_type=F32
        )
        for a in range(4):
            total = None
            for x in range(chunk):
                term = along[x * CUBE : (x + 1) * CUBE, :] * rows_g[a][x : x + 1, :]
                total = term if total is None else total + term
            s_ref[a] += total
        return 0

    lax.fori_loop(0, CUBE // chunk, step, 0)
    for at, (a, b) in enumerate(ROWS):
        share_ref[at : at + 1, :] = (
            jnp.sum(s_ref[a] * gy_ref[b], axis=0, keepdims=True) * SCALE**3
        )


def grid_part(info, external):
    vmem = pl.BlockSpec(memory_space=pltpu.VMEM)
    return pl.pallas_call(
        grid_kernel,
        out_shape=(
            jax.ShapeDtypeStruct(external.shape, F32),
            jax.ShapeDtypeStruct((16, 256), F32),
        ),
        in_specs=[vmem, vmem],
        out_specs=(vmem, vmem),
        scratch_shapes=[
            pltpu.VMEM((4, CUBE, 256), F32),
            pltpu.VMEM((4, CUBE, 256), F32),
            pltpu.VMEM((128, 256), F32),
            pltpu.VMEM((4, CUBE, 256), F32),
            pltpu.VMEM((4, CUBE, 256), F32),
        ],
        compiler_params=pltpu.CompilerParams(vmem_limit_bytes=16 * 2**20),
        cost_estimate=pl.CostEstimate(
            flops=2 * 2 * 6 * 1024 * 256 * 128, bytes_accessed=2 * 2**20, transcendentals=2**18
        ),
    )(info, external)


def collect_kernel(near_ref, next_ref, last_ref, far_ref, atoms_ref, mine_ref):
    col = lax.axis_index("col")
    y, x = col // 4, col % 4
    total = jnp.zeros((16, 128), F32)
    for ref, dx in ((near_ref, 0), (next_ref, 1), (last_ref, 3), (far_ref, 2)):
        for j in range(2):
            source = (y + j) % 2 * 4 + (x + dx) % 4
            total += pltpu.roll(ref[16 * j : 16 * j + 16, :], (source + 7) % 8 * 16, 1)
    atoms_ref[...] = total
    mine_ref[...] = pltpu.roll(total, (8 - col) % 8 * 16, 1)


def collect(parts):
    vmem = pl.BlockSpec(memory_space=pltpu.VMEM)
    out = jax.ShapeDtypeStruct((16, 128), F32)
    return pl.pallas_call(
        collect_kernel,
        out_shape=(out, out),
        in_specs=[vmem] * 4,
        out_specs=(vmem, vmem),
        compiler_params=pltpu.CompilerParams(vmem_limit_bytes=2 * 2**20),
        cost_estimate=pl.CostEstimate(flops=0, bytes_accessed=2**17, transcendentals=0),
    )(*parts)


def row_of(y, z, core):
    return (y % 2 * 8 + z % 8) * 2 + core % 2


SITES = [(y, z, core) for y in range(2) for z in range(8) for core in range(2)]
ACROSS_Y = [(row_of(*s), row_of(s[0] + 1, s[1], s[2])) for s in SITES]
ACROSS_CORES = [(row_of(*s), row_of(s[0], s[1], s[2] + 1)) for s in SITES]
ALONG_Z = [(row_of(*s), row_of(s[0], s[1] + 1 - 2 * s[2], s[2])) for s in SITES]
COLS = [(y, x) for y in range(2) for x in range(4)]


def col_pairs(dy, dx):
    return [(y * 4 + x, (y + dy) % 2 * 4 + (x + dx) % 4) for y, x in COLS]


def ring(axis, size, step):
    return [(i, (i + step) % size) for i in range(size)]


def from_neighbours(last, first, axis, size):
    before = lax.ppermute(last, axis, ring(axis, size, 1))
    after = lax.ppermute(first, axis, ring(axis, size, -1))
    return before, after


def shifted(info, line, amount):
    return info.at[line].add(amount)


def on_device(coefficients, off_x, off_y, off_z, external, pattern, hamiltonian, density_matrix):
    core = lax.axis_index("row") % 2
    hp, pp = pack(pattern, hamiltonian, density_matrix)
    table_p, table_h = tile_tables(pattern)

    coef = coefficients.reshape(4, 4, 2, 2, 4).transpose(3, 1, 2, 0, 4).reshape(16, 16)
    offs = jnp.stack([off_x, off_y, off_z]).astype(F32)
    offs = jnp.broadcast_to(offs[:, :, None], (3, 4, 4)).reshape(3, 16)
    info = jnp.concatenate([coef, offs, jnp.zeros((5, 16), F32)], axis=0)
    before, after = from_neighbours(info, info, "col", 8)
    info = jnp.concatenate([shifted(before, 17, -32.0), info, shifted(after, 17, 32.0)], axis=1)
    before, after = from_neighbours(info, info, "row", 32)
    info = jnp.concatenate(
        [shifted(before, 16, -32.0), info, shifted(after, 16, 32.0), jnp.zeros((24, 112), F32)], axis=1
    )
    density, share = grid_part(info, external)
    before, after = from_neighbours(share[:, 96:144], share[:, 0:48], "row", 32)
    share = share[:, 48:96] + before + after
    share = jnp.concatenate([share, jnp.zeros((16, 80), F32)], axis=1)
    other = lax.ppermute(share, "col", col_pairs(1, 0))
    share = jnp.concatenate([share, other], axis=0)
    shares = [share] + [lax.ppermute(share, "col", col_pairs(0, d)) for d in (3, 1, 2)]
    atoms, mine = collect(shares)
    integrals = (
        mine[:, :16].reshape(2, 4, 2, 4, 4).transpose(3, 1, 2, 0, 4).reshape(4, 64)
    )

    hy = lax.ppermute(hp, "col", col_pairs(1, 0))
    h0 = jnp.concatenate([hp, hy], axis=0)
    h_next = lax.ppermute(h0, "col", col_pairs(0, 3))
    h_last = lax.ppermute(h0, "col", col_pairs(0, 1))
    h_far = lax.ppermute(h0, "col", col_pairs(0, 2))
    h_dense = spread_hamiltonian(
        table_h, [h0, h_next, h_last, h_far], ((0, 0), (1, 1), (2, 3), (3, 2))
    )

    py = lax.ppermute(pp, "row", ACROSS_Y)
    m = jnp.concatenate([pp, py], axis=0)
    mc = lax.ppermute(m, "row", ACROSS_CORES)
    own = [m, mc]
    product = None
    chain, chain_c = m, mc
    for s in (1, 2, 3):
        chain = lax.ppermute(chain, "row", ALONG_Z)
        chain_c = lax.ppermute(chain_c, "row", ALONG_Z)
        other = lax.ppermute(chain, "row", ACROSS_CORES)
        other_c = lax.ppermute(chain_c, "row", ACROSS_CORES)
        product = accumulate(
            table_p,
            h_dense,
            product,
            [chain, chain_c, other, other_c],
            ((-s, 0), (-s, 1), (s, 1), (s, 0)),
        )
    chain = lax.ppermute(chain, "row", ALONG_Z)
    other = lax.ppermute(chain, "row", ACROSS_CORES)
    product = accumulate(table_p, h_dense, product, own, ((0, 0), (0, 1)), atoms)
    product = accumulate(table_p, h_dense, product, [chain, other], ((4, 0), (4, 1)))
    return (density, integrals, product)


def solution(mesh):
    return jax.shard_map(
        on_device,
        mesh=mesh,
        in_specs=(
            P(("row", "col"), None),
            P(("row", "col")),
            P(("row", "col")),
            P(("row", "col")),
            P("row", "col", None),
            P(),
            P("row", "col"),
            P("row", "col"),
        ),
        out_specs=(P("row", "col", None), P(("row", "col"), None), P("row", "col")),
        check_vma=False,
    )
```

```python
import functools

import jax
import jax.numpy as jnp
from jax import lax
from jax.experimental import pallas as pl
from jax.experimental.pallas import tpu as pltpu
from jax.sharding import PartitionSpec as P

BS = 64
CUBE = 32
SLOTS = 24
PACK = SLOTS // 2 * BS
F32 = jnp.float32
BF16 = jnp.bfloat16
PRECISE = lax.Precision.HIGHEST
SCALE = 6.0 / CUBE


def swap_halves(block):
    return jnp.concatenate([block[:, BS:], block[:, :BS]], axis=1)


def atom_rows(coef_ref, offset_refs, info_ref, wide):
    rho = lax.broadcasted_iota(jnp.int32, (16, 64), 0)
    lane = lax.broadcasted_iota(jnp.int32, (16, 64), 1)
    match = lane // 4 == rho % 8 // 2 * 4 + rho % 2 * 2 + rho // 8
    for i in range(4):
        wide[:, 64 * i : 64 * i + 64] = jnp.where(match, coef_ref[i : i + 1, :], 0.0)
    m = lax.broadcasted_iota(jnp.int32, (256, 128), 0)
    target = lax.broadcasted_iota(jnp.int32, (256, 128), 1)
    move = jnp.where((target // 4 == m // 64) & (target % 4 == m % 4), 1.0, 0.0)
    total = jnp.dot(wide[...], move, precision=PRECISE, preferred_element_type=F32)
    info_ref[0:16, :] = total[:, :16]
    atom = lax.broadcasted_iota(jnp.int32, (8, 16), 1) // 4
    line = lax.broadcasted_iota(jnp.int32, (8, 16), 0)
    lower = jnp.zeros((8, 16), F32)
    for k, ref in enumerate(offset_refs):
        for i in range(4):
            lower = jnp.where((line == k) & (atom == i), ref[i].astype(F32), lower)
    info_ref[16:24, :] = lower


def pack_kernel(
    pattern_hbm, h_hbm, p_hbm, coef_hbm, x_hbm, y_hbm, z_hbm, hp_ref, pp_ref, info_ref,
    rows, places, h_ref, p_ref, coef_ref, x_ref, y_ref, z_ref, wide, sems,
):
    row, col = lax.axis_index("row"), lax.axis_index("col")
    copies = [
        pltpu.make_async_copy(
            pattern_hbm.at[pl.ds(pl.multiple_of(row // 2 * 8, 8), 8), :], rows, sems.at[0]
        ),
        pltpu.make_async_copy(p_hbm, p_ref, sems.at[1]),
        pltpu.make_async_copy(h_hbm, h_ref, sems.at[2]),
        pltpu.make_async_copy(coef_hbm, coef_ref, sems.at[3]),
        pltpu.make_async_copy(x_hbm, x_ref, sems.at[4]),
        pltpu.make_async_copy(y_hbm, y_ref, sems.at[5]),
        pltpu.make_async_copy(z_hbm, z_ref, sems.at[6]),
    ]
    for copy in copies:
        copy.start()

    def clear(i, _):
        places[i] = 0
        return 0

    lax.fori_loop(0, SLOTS + 1, clear, 0)
    copies[0].wait()
    count = jnp.int32(0)
    for block in range(64):
        places[count] = block
        flag = rows[row % 2 * 4 + block // 16, col * 16 + block % 16]
        count = count + jnp.where(flag != 0, 1, 0)
    left = lax.broadcasted_iota(jnp.int32, (BS, 2 * BS), 1) < BS
    for copy, source, target in ((copies[1], p_ref, pp_ref), (copies[2], h_ref, hp_ref)):
        copy.wait()
        for pair in range(SLOTS // 2):
            halves = []
            for half in range(2):
                place = places[2 * pair + half]
                r, c = place // 16, place % 16
                block = source[
                    pl.ds(pl.multiple_of(r * BS, BS), BS),
                    pl.ds(pl.multiple_of(c // 2 * 128, 128), 128),
                ]
                halves.append(jnp.where(c % 2 == half, block, swap_halves(block)))
            target[pl.ds(pair * BS, BS), :] = jnp.where(left, halves[0], halves[1])
    for copy in copies[3:]:
        copy.wait()
    atom_rows(coef_ref, (x_ref, y_ref, z_ref), info_ref, wide)


def pack(*operands):
    packed = jax.ShapeDtypeStruct((PACK, 128), BF16)
    vmem = pl.BlockSpec(memory_space=pltpu.VMEM)
    return pl.pallas_call(
        pack_kernel,
        out_shape=(packed, packed, jax.ShapeDtypeStruct((24, 16), F32)),
        in_specs=[pl.BlockSpec(memory_space=pltpu.HBM)] * 7,
        out_specs=(vmem, vmem, vmem),
        scratch_shapes=[
            pltpu.SMEM((8, 128), jnp.int32),
            pltpu.SMEM((SLOTS + 8,), jnp.int32),
            pltpu.VMEM((256, 1024), BF16),
            pltpu.VMEM((256, 1024), BF16),
            pltpu.VMEM((4, 64), F32),
            pltpu.SMEM((4,), jnp.int32),
            pltpu.SMEM((4,), jnp.int32),
            pltpu.SMEM((4,), jnp.int32),
            pltpu.VMEM((16, 256), F32),
            pltpu.SemaphoreType.DMA((7,)),
        ],
        compiler_params=pltpu.CompilerParams(vmem_limit_bytes=58 * 2**20),
        cost_estimate=pl.CostEstimate(flops=0, bytes_accessed=6 * 2**20, transcendentals=0),
    )(*operands)


def offsets_of(slot, flags):
    slot = slot.astype(jnp.int32)
    parity = lax.broadcasted_iota(jnp.int32, slot.shape, 1) % 2
    at = slot // 2 * BS + jnp.where(slot % 2 == parity, 0, PACK)
    return jnp.where(flags > 0, at, 2 * PACK)


def table_kernel(pattern_ref, _, p_ref, h_ref, held):
    row, col = lax.axis_index("row"), lax.axis_index("col")
    r = lax.broadcasted_iota(jnp.int32, (128, 128), 0)
    m = lax.broadcasted_iota(jnp.int32, (128, 128), 1)

    def product(a, b):
        return jnp.dot(a.astype(BF16), b.astype(BF16), preferred_element_type=F32)

    def ones(where):
        return jnp.where(where, 1.0, 0.0)

    flags = ones(pattern_ref[...] != 0)
    mine = jnp.where(m < 16, pltpu.roll(flags, (8 - col) % 8 * 16, 1), 0.0)
    above = ones((r // 4 == m // 4) & (m < r))
    slot = product(mine, ones((r < m) & (m < 16)))
    slot += product(above, product(mine, ones(r < 16)))
    held[...] = offsets_of(slot, mine)
    total = jnp.zeros((32, 128), jnp.int32)
    lane = lax.broadcasted_iota(jnp.int32, (32, 128), 1)
    for b in range(4):
        part = jnp.where(lane < 16, held[pl.ds(b, 32, stride=4), :], 0)
        total += pltpu.roll(part, 16 * b, 1) if b else part
    p_ref[...] = total[:, :64]

    two = ones(pattern_ref[pl.ds(pl.multiple_of(row // 2 * 8, 8), 8), :] != 0)
    two = jnp.where(row % 2 == 0, two, pltpu.roll(two, 4, 0))
    four = jnp.where(lax.broadcasted_iota(jnp.int32, (8, 128), 0) < 4, two, 0.0)
    before = product(four, ones((r // 16 == m // 16) & (r < m)))
    whole = product(four, ones(r // 16 == m // 16))
    up = lax.broadcasted_iota(jnp.int32, (8, 8), 1) < lax.broadcasted_iota(jnp.int32, (8, 8), 0)
    before += jnp.dot(ones(up), whole, precision=PRECISE, preferred_element_type=F32)
    h_ref[...] = offsets_of(before, four)


def tile_tables(pattern, after):
    vmem = pl.BlockSpec(memory_space=pltpu.VMEM)
    return pl.pallas_call(
        table_kernel,
        out_shape=(
            jax.ShapeDtypeStruct((32, 64), jnp.int32),
            jax.ShapeDtypeStruct((8, 128), jnp.int32),
        ),
        in_specs=[vmem, pl.BlockSpec(memory_space=pl.ANY)],
        out_specs=(vmem, vmem),
        scratch_shapes=[pltpu.VMEM((128, 128), jnp.int32)],
        compiler_params=pltpu.CompilerParams(vmem_limit_bytes=4 * 2**20),
        cost_estimate=pl.CostEstimate(flops=0, bytes_accessed=2**21, transcendentals=0),
    )(pattern, after)


def spread_tile(packed, offset, both, store):
    both[0:PACK, :] = packed
    both[PACK : 2 * PACK, :] = swap_halves(packed)
    left = lax.broadcasted_iota(jnp.int32, (BS, 2 * BS), 1) < BS
    for r in range(4):
        for c in range(8):
            at0 = pl.multiple_of(offset(r, 2 * c), BS)
            at1 = pl.multiple_of(offset(r, 2 * c + 1), BS)
            block = jnp.where(left, both[pl.ds(at0, BS), :], both[pl.ds(at1, BS), :])
            store(r, c, block)


def spread_kernel(table_ref, near_ref, next_ref, last_ref, far_ref, out_ref, both):
    col = lax.axis_index("col")
    y, x = col // 4, col % 4
    both[2 * PACK :, :] = jnp.zeros((BS, 128), BF16)
    for part, dx in ((near_ref, 0), (next_ref, 1), (last_ref, 3), (far_ref, 2)):

        def one(j, _, part=part, dx=dx):
            source = (y + j) % 2 * 4 + (x + dx) % 4
            packed = part[pl.ds(pl.multiple_of(j * PACK, PACK), PACK), :]

            def store(r, c, block):
                out_ref[
                    source * 4 + c // 2, r * BS : (r + 1) * BS, c % 2 * 128 : c % 2 * 128 + 128
                ] = block

            spread_tile(packed, lambda r, c: table_ref[r, source * 16 + c], both, store)
            return 0

        lax.fori_loop(0, 2, one, 0)


def spread_hamiltonian(table, parts):
    vmem = pl.BlockSpec(memory_space=pltpu.VMEM)
    return pl.pallas_call(
        spread_kernel,
        out_shape=jax.ShapeDtypeStruct((32, 256, 256), BF16),
        in_specs=[pl.BlockSpec(memory_space=pltpu.SMEM)] + [vmem] * len(parts),
        out_specs=vmem,
        scratch_shapes=[pltpu.VMEM((2 * PACK + BS, 128), BF16)],
        compiler_params=pltpu.CompilerParams(vmem_limit_bytes=4 * 2**20),
        cost_estimate=pl.CostEstimate(flops=0, bytes_accessed=8 * 2**20, transcendentals=0),
    )(table, *parts)


def split3(value):
    high = value.astype(BF16)
    rest = value - high.astype(F32)
    middle = rest.astype(BF16)
    return high, middle, (rest - middle.astype(F32)).astype(BF16)


def accumulate_kernel(groups, start, local, after, table_ref, h_ref, *refs):
    refs = list(refs)
    before = None if start else refs.pop(0)
    atoms, mine = (refs.pop(0), refs.pop(0)) if local else (None, None)
    parts = [refs.pop(0) for _ in groups]
    if after:
        refs.pop(0)
    out_ref, token_ref, both, dense, wide, table, sem = refs[:7]
    token_ref[...] = jnp.zeros_like(token_ref)
    copy = pltpu.make_async_copy(table_ref, table, sem)
    copy.start()
    row = lax.axis_index("row")
    y, z, core = row // 16, row // 2 % 8, row % 2
    direction = 1 - 2 * core
    both[2 * PACK :, :] = jnp.zeros((BS, 128), BF16)
    tiles = []
    for steps, flip in groups:
        for j in range(2):
            tiles.append(((y + j) % 2 * 8 + (z + steps * direction + 8) % 8) * 2 + (core + flip) % 2)
    for at, tile in enumerate(tiles):
        wide[:, at * 256 : at * 256 + 256] = h_ref[tile]
    copy.wait()
    for g, part in enumerate(parts):

        def one(j, _, part=part, g=g):
            tile = jnp.where(j == 0, tiles[2 * g], tiles[2 * g + 1])
            packed = part[pl.ds(pl.multiple_of(j * PACK, PACK), PACK), :]
            base = pl.multiple_of((2 * g + j) * 256, 256)

            def store(r, c, block):
                dense[pl.ds(base + r * BS, BS), c * 128 : c * 128 + 128] = block

            spread_tile(packed, lambda r, c: table[tile, r * 16 + c], both, store)
            return 0

        lax.fori_loop(0, 2, one, 0)
    if local:
        own, held = refs[7], refs[8]

        def store(r, c, block):
            own[r * BS : r * BS + BS, c * 128 : c * 128 + 128] = block

        spread_tile(mine[0:PACK, :], lambda r, c: table[row, r * 16 + c], both, store)
        values = atoms[...]
        lane_atom = lax.broadcasted_iota(jnp.int32, (256, 128), 1) // 4
        row_atom = lax.broadcasted_iota(jnp.int32, (256, 128), 0) // 8
        tall = [
            jnp.where(
                lane_atom == row_atom,
                jnp.concatenate([values[8 * b : 8 * b + 8, :]] * 32, axis=0),
                0.0,
            )
            for b in range(2)
        ]
        q = lax.broadcasted_iota(jnp.int32, (256, 256), 0)
        m = lax.broadcasted_iota(jnp.int32, (256, 256), 1)
        place = q % 128 // 4 * 8 + q // 128 * 4 + q % 4
        chosen = jnp.where(place == m, 1.0, 0.0).astype(BF16)
        for k, t in enumerate(split3(jnp.concatenate(tall, axis=1))):
            held[k] = jnp.dot(t, chosen, preferred_element_type=F32).astype(BF16)

    def column(n, _):
        lanes = pl.ds(pl.multiple_of(n * 256, 256), 256)
        total = jnp.dot(wide[...], dense[:, lanes], preferred_element_type=F32)
        if local:
            for k in range(3):
                total += jnp.dot(held[k], own[:, lanes], preferred_element_type=F32)
        if before is not None:
            total += before[:, lanes]
        out_ref[:, lanes] = total
        return 0

    lax.fori_loop(0, 4, column, 0)


def accumulate(table, h_dense, before, parts, groups, local=(), after=None):
    vmem = pl.BlockSpec(memory_space=pltpu.VMEM)
    operands = [h_dense]
    if before is not None:
        operands.append(before)
    operands += list(local) + parts
    specs = [pl.BlockSpec(memory_space=pl.ANY)] + [vmem] * len(operands)
    if after is not None:
        operands.append(after)
        specs.append(pl.BlockSpec(memory_space=pl.ANY))
    depth = 512 * len(groups)
    scratch = [
        pltpu.VMEM((2 * PACK + BS, 128), BF16),
        pltpu.VMEM((depth, 1024), BF16),
        pltpu.VMEM((256, depth), BF16),
        pltpu.SMEM((32, 64), jnp.int32),
        pltpu.SemaphoreType.DMA,
    ]
    if local:
        scratch += [pltpu.VMEM((256, 1024), BF16), pltpu.VMEM((3, 256, 256), BF16)]
    return pl.pallas_call(
        functools.partial(accumulate_kernel, groups, before is None, bool(local), after is not None),
        out_shape=(jax.ShapeDtypeStruct((256, 1024), F32), jax.ShapeDtypeStruct((8, 128), F32)),
        in_specs=specs,
        out_specs=(vmem, vmem),
        scratch_shapes=scratch,
        compiler_params=pltpu.CompilerParams(vmem_limit_bytes=12 * 2**20),
        cost_estimate=pl.CostEstimate(
            flops=4 * 256 * 512 * 1024 * len(groups), bytes_accessed=4 * 2**20 * len(groups), transcendentals=0
        ),
    )(table, *operands)


def tie(buffer, token):
    anywhere = pl.BlockSpec(memory_space=pl.ANY)

    def kernel(buffer_ref, token_ref, out_ref):
        pass

    return pl.pallas_call(
        kernel,
        out_shape=jax.ShapeDtypeStruct(buffer.shape, buffer.dtype),
        in_specs=[anywhere, anywhere],
        out_specs=anywhere,
        input_output_aliases={0: 0},
        compiler_params=pltpu.CompilerParams(vmem_limit_bytes=2**20),
        cost_estimate=pl.CostEstimate(flops=0, bytes_accessed=0, transcendentals=0),
    )(buffer, token)


def hermite(distance):
    scaled = (distance + (0.5 - CUBE / 2.0)) * SCALE
    inside = (distance >= 0) & (distance < CUBE)
    gaussian = jnp.where(inside, jnp.exp(-0.5 * scaled * scaled), 0.0)
    return gaussian, scaled


def powers(distance):
    gaussian, scaled = hermite(distance)
    first = scaled * gaussian
    second = scaled * first
    return gaussian, first, second, scaled * second


ROWS = [(a, 2 * bh + bl) for bl in range(2) for a in range(4) for bh in range(2)]


def grid_kernel(info_ref, external_hbm, density_ref, share_ref, gx_ref, gy_ref, gz_ref, u_ref, s_ref, external_ref, sem):
    lanes = 256
    copy = pltpu.make_async_copy(external_hbm, external_ref, sem)
    copy.start()
    cell = lax.broadcasted_iota(jnp.int32, (CUBE, lanes), 0).astype(F32)
    place = lax.broadcasted_iota(jnp.int32, (1, lanes), 1)
    off_x = info_ref[16:17, :] + CUBE * (place // 48 - 1).astype(F32)
    off_y = info_ref[17:18, :] + CUBE * (place % 48 // 16 - 1).astype(F32)
    off_z = info_ref[18:19, :]
    for n, value in enumerate(powers(cell - off_x + CUBE // 2)):
        gx_ref[n] = value
    for n, value in enumerate(powers(cell - off_y + CUBE // 2)):
        gy_ref[n] = value
    deep = lax.broadcasted_iota(jnp.int32, (128, lanes), 0).astype(F32)
    away = deep - off_z + CUBE // 2
    away = jnp.where(away < 0, away + 128.0, away)
    away = jnp.where(away >= 128, away - 128.0, away)
    kinds = powers(away)
    e = lax.broadcasted_iota(jnp.int32, (128, lanes), 1) % 4
    gz_ref[...] = jnp.where(e == 0, kinds[0], jnp.where(e == 1, kinds[1], jnp.where(e == 2, kinds[2], kinds[3])))
    for b in range(4):
        total = None
        for a in range(4):
            at = ROWS.index((a, b))
            term = info_ref[at : at + 1, :] * gx_ref[a]
            total = term if total is None else total + term
        u_ref[b] = total
    s_ref[...] = jnp.zeros_like(s_ref)
    gz = gz_ref[...]
    chunk = 8
    copy.wait()

    def step(i, _):
        planes = []
        x0 = pl.multiple_of(i * chunk, chunk)
        rows_u = [u_ref[b, pl.ds(x0, chunk), :] for b in range(4)]
        rows_g = [gx_ref[a, pl.ds(x0, chunk), :] for a in range(4)]
        for x in range(chunk):
            plane = None
            for b in range(4):
                term = rows_u[b][x : x + 1, :] * gy_ref[b]
                plane = term if plane is None else plane + term
            planes.append(plane)
        spread = jnp.concatenate(planes, axis=0)
        density = lax.dot_general(
            spread, gz, (((1,), (1,)), ((), ())), precision=PRECISE, preferred_element_type=F32
        )
        density = density.reshape(chunk, CUBE, 128)
        density_ref[pl.ds(x0, chunk)] = density
        potential = external_ref[pl.ds(x0, chunk)] + jnp.tanh(density)
        along = jnp.dot(
            potential.reshape(chunk * CUBE, 128), gz, precision=PRECISE, preferred_element_type=F32
        )
        for a in range(4):
            total = None
            for x in range(chunk):
                term = along[x * CUBE : (x + 1) * CUBE, :] * rows_g[a][x : x + 1, :]
                total = term if total is None else total + term
            s_ref[a] += total
        return 0

    lax.fori_loop(0, CUBE // chunk, step, 0)
    for at, (a, b) in enumerate(ROWS):
        share_ref[at : at + 1, :] = (
            jnp.sum(s_ref[a] * gy_ref[b], axis=0, keepdims=True) * SCALE**3
        )


def grid_part(info, external):
    vmem = pl.BlockSpec(memory_space=pltpu.VMEM)
    return pl.pallas_call(
        grid_kernel,
        out_shape=(
            jax.ShapeDtypeStruct(external.shape, F32),
            jax.ShapeDtypeStruct((16, 256), F32),
        ),
        in_specs=[vmem, pl.BlockSpec(memory_space=pltpu.HBM)],
        out_specs=(vmem, vmem),
        scratch_shapes=[
            pltpu.VMEM((4, CUBE, 256), F32),
            pltpu.VMEM((4, CUBE, 256), F32),
            pltpu.VMEM((128, 256), F32),
            pltpu.VMEM((4, CUBE, 256), F32),
            pltpu.VMEM((4, CUBE, 256), F32),
            pltpu.VMEM(external.shape, F32),
            pltpu.SemaphoreType.DMA,
        ],
        compiler_params=pltpu.CompilerParams(vmem_limit_bytes=12 * 2**20),
        cost_estimate=pl.CostEstimate(
            flops=2 * 2 * 6 * 1024 * 256 * 128, bytes_accessed=2 * 2**20, transcendentals=2**18
        ),
    )(info, external)


def collect_kernel(near_ref, next_ref, last_ref, far_ref, atoms_ref, mine_ref):
    col = lax.axis_index("col")
    y, x = col // 4, col % 4
    total = jnp.zeros((16, 128), F32)
    for ref, dx in ((near_ref, 0), (next_ref, 1), (last_ref, 3), (far_ref, 2)):
        for j in range(2):
            source = (y + j) % 2 * 4 + (x + dx) % 4
            total += pltpu.roll(ref[16 * j : 16 * j + 16, :], (source + 7) % 8 * 16, 1)
    atoms_ref[...] = total
    mine = pltpu.roll(total, (8 - col) % 8 * 16, 1)
    lane = lax.broadcasted_iota(jnp.int32, (16, 128), 1)
    l = lax.broadcasted_iota(jnp.int32, (128, 64), 0)
    m = lax.broadcasted_iota(jnp.int32, (128, 64), 1)
    move = jnp.where(l % 4 == m % 4, 1.0, 0.0)
    rho = lax.broadcasted_iota(jnp.int32, (16, 64), 0)
    match = lax.broadcasted_iota(jnp.int32, (16, 64), 1) // 4 == rho % 8 // 2 * 4 + rho % 2 * 2 + rho // 8
    for i in range(4):
        value = jnp.dot(
            jnp.where(lane // 4 == i, mine, 0.0), move, precision=PRECISE, preferred_element_type=F32
        )
        mine_ref[i : i + 1, :] = jnp.sum(jnp.where(match, value, 0.0), axis=0, keepdims=True)


def collect(parts):
    vmem = pl.BlockSpec(memory_space=pltpu.VMEM)
    return pl.pallas_call(
        collect_kernel,
        out_shape=(jax.ShapeDtypeStruct((16, 128), F32), jax.ShapeDtypeStruct((4, 64), F32)),
        in_specs=[vmem] * 4,
        out_specs=(vmem, vmem),
        compiler_params=pltpu.CompilerParams(vmem_limit_bytes=2 * 2**20),
        cost_estimate=pl.CostEstimate(flops=0, bytes_accessed=2**17, transcendentals=0),
    )(*parts)


def row_of(y, z, core):
    return (y % 2 * 8 + z % 8) * 2 + core % 2


SITES = [(y, z, core) for y in range(2) for z in range(8) for core in range(2)]
ACROSS_Y = [(row_of(*s), row_of(s[0] + 1, s[1], s[2])) for s in SITES]
ACROSS_CORES = [(row_of(*s), row_of(s[0], s[1], s[2] + 1)) for s in SITES]
ALONG_Z = [(row_of(*s), row_of(s[0], s[1] + 1 - 2 * s[2], s[2])) for s in SITES]
COLS = [(y, x) for y in range(2) for x in range(4)]


def col_pairs(dy, dx):
    return [(y * 4 + x, (y + dy) % 2 * 4 + (x + dx) % 4) for y, x in COLS]


ALONG_X = [
    (r * 8 + y * 4 + x, r * 8 + y * 4 + (x + 1 - 2 * (r % 2)) % 4) for r in range(32) for y, x in COLS
]


def ring(axis, size, step):
    return [(i, (i + step) % size) for i in range(size)]


def from_neighbours(last, first, axis, size):
    before = lax.ppermute(last, axis, ring(axis, size, 1))
    after = lax.ppermute(first, axis, ring(axis, size, -1))
    return before, after


def on_device(coefficients, off_x, off_y, off_z, external, pattern, hamiltonian, density_matrix):
    core = lax.axis_index("row") % 2
    hp, pp, info = pack(
        pattern, hamiltonian, density_matrix, coefficients, off_x, off_y, off_z
    )
    table_p, table_h = tile_tables(pattern, info)

    before, after = from_neighbours(info, info, "col", 8)
    info = jnp.concatenate([before, info, after], axis=1)
    before, after = from_neighbours(info, info, "row", 32)
    info = jnp.concatenate([before, info, after, jnp.zeros((24, 112), F32)], axis=1)
    density, share9 = grid_part(info, external)
    share = share9
    before, after = from_neighbours(share[:, 96:144], share[:, 0:48], "row", 32)
    share = share[:, 48:96] + before + after
    share = jnp.concatenate([share, jnp.zeros((16, 80), F32)], axis=1)
    other = lax.ppermute(share, "col", col_pairs(1, 0))
    share = jnp.concatenate([share, other], axis=0)
    shares = [share] + [lax.ppermute(share, "col", col_pairs(0, d)) for d in (3, 1, 2)]
    atoms, integrals = collect(shares)

    hy = lax.ppermute(hp, "col", col_pairs(1, 0))
    h0 = jnp.concatenate([hp, hy], axis=0)
    h_next = lax.ppermute(h0, "col", col_pairs(0, 3))
    h_last = lax.ppermute(h0, "col", col_pairs(0, 1))
    h_far = lax.ppermute(jnp.where(core == 0, h_last, h_next), ("row", "col"), ALONG_X)
    h_dense = spread_hamiltonian(table_h, [h0, h_next, h_last, h_far])

    py = lax.ppermute(pp, "row", ACROSS_Y)
    m = jnp.concatenate([pp, py], axis=0)
    mc = lax.ppermute(m, "row", ACROSS_CORES)

    def step(chain):
        chain = lax.ppermute(chain, "row", ALONG_Z)
        return chain, lax.ppermute(chain, "row", ACROSS_CORES)

    def groups(s):
        return ((-s, 0), (-s, 1), (s, 1), (s, 0))

    m1, x1 = step(m)
    c1, xc1 = step(mc)
    m2, x2 = step(m1)
    c2 = lax.ppermute(c1, "row", ALONG_Z)
    product, done = accumulate(
        table_p,
        h_dense,
        None,
        [m, mc, m1, c1, x1, xc1],
        ((0, 0), (0, 1)) + groups(1),
        after=share9,
    )
    c2 = tie(c2, done)
    xc2 = lax.ppermute(c2, "row", ACROSS_CORES)
    c3, xc3 = step(c2)
    m3 = lax.ppermute(m2, "row", ALONG_Z)
    product, done = accumulate(
        table_p, h_dense, product, [m2, c2, x2, xc2], groups(2), after=share
    )
    m3 = tie(m3, done)
    x3 = lax.ppermute(m3, "row", ACROSS_CORES)
    m4, x4 = step(m3)
    product, _ = accumulate(
        table_p, h_dense, product, [m3, c3, x3, xc3], groups(3), local=(atoms, pp)
    )
    product, _ = accumulate(table_p, h_dense, product, [m4, x4], ((4, 0), (4, 1)))
    return (density, integrals, product)


def solution(mesh):
    return jax.shard_map(
        on_device,
        mesh=mesh,
        in_specs=(
            P(("row", "col"), None),
            P(("row", "col")),
            P(("row", "col")),
            P(("row", "col")),
            P("row", "col", None),
            P(),
            P("row", "col"),
            P("row", "col"),
        ),
        out_specs=(P("row", "col", None), P(("row", "col"), None), P("row", "col")),
        check_vma=False,
    )
```

```python
import functools

import jax
import jax.numpy as jnp
from jax import lax
from jax.experimental import pallas as pl
from jax.experimental.pallas import tpu as pltpu
from jax.sharding import PartitionSpec as P

BS = 64
CUBE = 32
SLOTS = 24
PACK = SLOTS // 2 * BS
F32 = jnp.float32
BF16 = jnp.bfloat16
PRECISE = lax.Precision.HIGHEST
SCALE = 6.0 / CUBE
FREE = pl.CostEstimate(flops=0, bytes_accessed=0, transcendentals=0)


def swap_halves(block):
    return jnp.concatenate([block[:, BS:], block[:, :BS]], axis=1)


def atom_rows(coef_ref, offset_refs, info_ref, wide):
    rho = lax.broadcasted_iota(jnp.int32, (16, 64), 0)
    lane = lax.broadcasted_iota(jnp.int32, (16, 64), 1)
    match = lane // 4 == rho % 8 // 2 * 4 + rho % 2 * 2 + rho // 8
    for i in range(4):
        wide[:, 64 * i : 64 * i + 64] = jnp.where(match, coef_ref[i : i + 1, :], 0.0)
    m = lax.broadcasted_iota(jnp.int32, (256, 128), 0)
    target = lax.broadcasted_iota(jnp.int32, (256, 128), 1)
    move = jnp.where((target // 4 == m // 64) & (target % 4 == m % 4), 1.0, 0.0)
    total = jnp.dot(wide[...], move, precision=PRECISE, preferred_element_type=F32)
    info_ref[0:16, :] = total[:, :16]
    atom = lax.broadcasted_iota(jnp.int32, (8, 16), 1) // 4
    line = lax.broadcasted_iota(jnp.int32, (8, 16), 0)
    lower = jnp.zeros((8, 16), F32)
    for k, ref in enumerate(offset_refs):
        for i in range(4):
            lower = jnp.where((line == k) & (atom == i), ref[i].astype(F32), lower)
    info_ref[16:24, :] = lower


def pack_kernel(
    pattern_hbm, h_hbm, p_hbm, coef_hbm, x_hbm, y_hbm, z_hbm, hp_ref, pp_ref, info_ref,
    rows, places, h_ref, p_ref, coef_ref, x_ref, y_ref, z_ref, wide, sems,
):
    row, col = lax.axis_index("row"), lax.axis_index("col")
    copies = [
        pltpu.make_async_copy(
            pattern_hbm.at[pl.ds(pl.multiple_of(row // 2 * 8, 8), 8), :], rows, sems.at[0]
        ),
        pltpu.make_async_copy(p_hbm, p_ref, sems.at[1]),
        pltpu.make_async_copy(h_hbm, h_ref, sems.at[2]),
        pltpu.make_async_copy(coef_hbm, coef_ref, sems.at[3]),
        pltpu.make_async_copy(x_hbm, x_ref, sems.at[4]),
        pltpu.make_async_copy(y_hbm, y_ref, sems.at[5]),
        pltpu.make_async_copy(z_hbm, z_ref, sems.at[6]),
    ]
    for copy in copies:
        copy.start()

    def clear(i, _):
        places[i] = 0
        return 0

    lax.fori_loop(0, SLOTS + 1, clear, 0)
    copies[0].wait()
    count = jnp.int32(0)
    for block in range(64):
        places[count] = block
        flag = rows[row % 2 * 4 + block // 16, col * 16 + block % 16]
        count = count + jnp.where(flag != 0, 1, 0)
    left = lax.broadcasted_iota(jnp.int32, (BS, 2 * BS), 1) < BS
    for copy, source, target in ((copies[1], p_ref, pp_ref), (copies[2], h_ref, hp_ref)):
        copy.wait()
        for at in range(0, SLOTS // 2, 4):
            blocks = []
            for pair in range(at, at + 4):
                halves = []
                for half in range(2):
                    place = places[2 * pair + half]
                    r, c = place // 16, place % 16
                    block = source[
                        pl.ds(pl.multiple_of(r * BS, BS), BS),
                        pl.ds(pl.multiple_of(c // 2 * 128, 128), 128),
                    ]
                    halves.append(jnp.where(c % 2 == half, block, swap_halves(block)))
                blocks.append(jnp.where(left, halves[0], halves[1]))
            for k, block in enumerate(blocks):
                target[pl.ds((at + k) * BS, BS), :] = block
    for copy in copies[3:]:
        copy.wait()
    atom_rows(coef_ref, (x_ref, y_ref, z_ref), info_ref, wide)


def pack(*operands):
    packed = jax.ShapeDtypeStruct((PACK, 128), BF16)
    vmem = pl.BlockSpec(memory_space=pltpu.VMEM)
    return pl.pallas_call(
        pack_kernel,
        out_shape=(packed, packed, jax.ShapeDtypeStruct((24, 16), F32)),
        in_specs=[pl.BlockSpec(memory_space=pltpu.HBM)] * 7,
        out_specs=(vmem, vmem, vmem),
        scratch_shapes=[
            pltpu.SMEM((8, 128), jnp.int32),
            pltpu.SMEM((SLOTS + 8,), jnp.int32),
            pltpu.VMEM((256, 1024), BF16),
            pltpu.VMEM((256, 1024), BF16),
            pltpu.VMEM((4, 64), F32),
            pltpu.SMEM((4,), jnp.int32),
            pltpu.SMEM((4,), jnp.int32),
            pltpu.SMEM((4,), jnp.int32),
            pltpu.VMEM((16, 256), F32),
            pltpu.SemaphoreType.DMA((7,)),
        ],
        compiler_params=pltpu.CompilerParams(vmem_limit_bytes=58 * 2**20),
        cost_estimate=FREE,
    )(*operands)


def offsets_of(slot, flags):
    slot = slot.astype(jnp.int32)
    parity = lax.broadcasted_iota(jnp.int32, slot.shape, 1) % 2
    at = slot // 2 * BS + jnp.where(slot % 2 == parity, 0, PACK)
    return jnp.where(flags > 0, at, 2 * PACK)


def table_kernel(pattern_ref, p_ref, h_ref, held):
    row, col = lax.axis_index("row"), lax.axis_index("col")
    r = lax.broadcasted_iota(jnp.int32, (128, 128), 0)
    m = lax.broadcasted_iota(jnp.int32, (128, 128), 1)

    def product(a, b):
        return jnp.dot(a.astype(BF16), b.astype(BF16), preferred_element_type=F32)

    def ones(where):
        return jnp.where(where, 1.0, 0.0)

    flags = ones(pattern_ref[...] != 0)
    mine = jnp.where(m < 16, pltpu.roll(flags, (8 - col) % 8 * 16, 1), 0.0)
    above = ones((r // 4 == m // 4) & (m < r))
    slot = product(mine, ones((r < m) & (m < 16)))
    slot += product(above, product(mine, ones(r < 16)))
    held[...] = offsets_of(slot, mine)
    total = jnp.zeros((32, 128), jnp.int32)
    lane = lax.broadcasted_iota(jnp.int32, (32, 128), 1)
    for b in range(4):
        part = jnp.where(lane < 16, held[pl.ds(b, 32, stride=4), :], 0)
        total += pltpu.roll(part, 16 * b, 1) if b else part
    p_ref[...] = total[:, :64]

    two = ones(pattern_ref[pl.ds(pl.multiple_of(row // 2 * 8, 8), 8), :] != 0)
    two = jnp.where(row % 2 == 0, two, pltpu.roll(two, 4, 0))
    four = jnp.where(lax.broadcasted_iota(jnp.int32, (8, 128), 0) < 4, two, 0.0)
    before = product(four, ones((r // 16 == m // 16) & (r < m)))
    whole = product(four, ones(r // 16 == m // 16))
    up = lax.broadcasted_iota(jnp.int32, (8, 8), 1) < lax.broadcasted_iota(jnp.int32, (8, 8), 0)
    before += jnp.dot(ones(up), whole, precision=PRECISE, preferred_element_type=F32)
    h_ref[...] = offsets_of(before, four)


def tile_tables(pattern):
    vmem = pl.BlockSpec(memory_space=pltpu.VMEM)
    return pl.pallas_call(
        table_kernel,
        out_shape=(
            jax.ShapeDtypeStruct((32, 64), jnp.int32),
            jax.ShapeDtypeStruct((8, 128), jnp.int32),
        ),
        in_specs=[vmem],
        out_specs=(vmem, vmem),
        scratch_shapes=[pltpu.VMEM((128, 128), jnp.int32)],
        compiler_params=pltpu.CompilerParams(vmem_limit_bytes=4 * 2**20),
        cost_estimate=FREE,
    )(pattern)


def spread_tile(packed, offset, both, store):
    both[0:PACK, :] = packed
    both[PACK : 2 * PACK, :] = swap_halves(packed)
    left = lax.broadcasted_iota(jnp.int32, (BS, 2 * BS), 1) < BS
    for r in range(4):
        for first in (0, 4):
            blocks = []
            for c in range(first, first + 4):
                at0 = pl.multiple_of(offset(r, 2 * c), BS)
                at1 = pl.multiple_of(offset(r, 2 * c + 1), BS)
                blocks.append(jnp.where(left, both[pl.ds(at0, BS), :], both[pl.ds(at1, BS), :]))
            for k, block in enumerate(blocks):
                store(r, first + k, block)


def spread_kernel(table_ref, near_ref, next_ref, last_ref, far_ref, out_ref, both):
    col = lax.axis_index("col")
    y, x = col // 4, col % 4
    both[2 * PACK :, :] = jnp.zeros((BS, 128), BF16)
    for part, dx in ((near_ref, 0), (next_ref, 1), (last_ref, 3), (far_ref, 2)):

        def one(j, _, part=part, dx=dx):
            source = (y + j) % 2 * 4 + (x + dx) % 4
            packed = part[pl.ds(pl.multiple_of(j * PACK, PACK), PACK), :]

            def store(r, c, block):
                out_ref[
                    source * 4 + c // 2, r * BS : (r + 1) * BS, c % 2 * 128 : c % 2 * 128 + 128
                ] = block

            spread_tile(packed, lambda r, c: table_ref[r, source * 16 + c], both, store)
            return 0

        lax.fori_loop(0, 2, one, 0)


def spread_hamiltonian(table, parts):
    vmem = pl.BlockSpec(memory_space=pltpu.VMEM)
    return pl.pallas_call(
        spread_kernel,
        out_shape=jax.ShapeDtypeStruct((32, 256, 256), BF16),
        in_specs=[pl.BlockSpec(memory_space=pltpu.SMEM)] + [vmem] * len(parts),
        out_specs=vmem,
        scratch_shapes=[pltpu.VMEM((2 * PACK + BS, 128), BF16)],
        compiler_params=pltpu.CompilerParams(vmem_limit_bytes=4 * 2**20),
        cost_estimate=FREE,
    )(table, *parts)


def split3(value):
    high = value.astype(BF16)
    rest = value - high.astype(F32)
    middle = rest.astype(BF16)
    return high, middle, (rest - middle.astype(F32)).astype(BF16)


def accumulate_kernel(groups, start, local, after, table_ref, h_ref, *refs):
    refs = list(refs)
    before = None if start else refs.pop(0)
    atoms, mine = (refs.pop(0), refs.pop(0)) if local else (None, None)
    parts = [refs.pop(0) for _ in groups]
    if after:
        refs.pop(0)
    out_ref, token_ref, both, dense, wide, table, sem = refs[:7]
    token_ref[...] = jnp.zeros_like(token_ref)
    copy = pltpu.make_async_copy(table_ref, table, sem)
    copy.start()
    row = lax.axis_index("row")
    y, z, core = row // 16, row // 2 % 8, row % 2
    direction = 1 - 2 * core
    both[2 * PACK :, :] = jnp.zeros((BS, 128), BF16)
    tiles = []
    for count, steps, flip in groups:
        for j in range(count):
            tiles.append(
                ((y + j) % 2 * 8 + (z + steps * direction + 8) % 8) * 2 + (core + flip + j // 2) % 2
            )
    for at, tile in enumerate(tiles):
        wide[:, at * 256 : at * 256 + 256] = h_ref[tile]
    copy.wait()
    start_at = 0
    for part, (count, _, _) in zip(parts, groups):

        def one(j, _, part=part, start_at=start_at, count=count):
            tile = tiles[start_at]
            for k in range(1, count):
                tile = jnp.where(j == k, tiles[start_at + k], tile)
            packed = part[pl.ds(pl.multiple_of(j * PACK, PACK), PACK), :]
            base = pl.multiple_of((start_at + j) * 256, 256)

            def store(r, c, block):
                dense[pl.ds(base + r * BS, BS), c * 128 : c * 128 + 128] = block

            spread_tile(packed, lambda r, c: table[tile, r * 16 + c], both, store)
            return 0

        lax.fori_loop(0, count, one, 0)
        start_at += count
    if local:
        own, held = refs[7], refs[8]

        def store(r, c, block):
            own[r * BS : r * BS + BS, c * 128 : c * 128 + 128] = block

        spread_tile(mine[0:PACK, :], lambda r, c: table[row, r * 16 + c], both, store)
        values = atoms[...]
        lane_atom = lax.broadcasted_iota(jnp.int32, (256, 128), 1) // 4
        row_atom = lax.broadcasted_iota(jnp.int32, (256, 128), 0) // 8
        tall = [
            jnp.where(
                lane_atom == row_atom,
                jnp.concatenate([values[8 * b : 8 * b + 8, :]] * 32, axis=0),
                0.0,
            )
            for b in range(2)
        ]
        q = lax.broadcasted_iota(jnp.int32, (256, 256), 0)
        m = lax.broadcasted_iota(jnp.int32, (256, 256), 1)
        place = q % 128 // 4 * 8 + q // 128 * 4 + q % 4
        chosen = jnp.where(place == m, 1.0, 0.0).astype(BF16)
        for k, t in enumerate(split3(jnp.concatenate(tall, axis=1))):
            held[k] = jnp.dot(t, chosen, preferred_element_type=F32).astype(BF16)

    def column(n, _):
        lanes = pl.ds(pl.multiple_of(n * 256, 256), 256)
        total = jnp.dot(wide[...], dense[:, lanes], preferred_element_type=F32)
        if local:
            for k in range(3):
                total += jnp.dot(held[k], own[:, lanes], preferred_element_type=F32)
        if before is not None:
            total += before[:, lanes]
        out_ref[:, lanes] = total
        return 0

    lax.fori_loop(0, 4, column, 0)


def accumulate(table, h_dense, before, parts, groups, local=(), after=None):
    vmem = pl.BlockSpec(memory_space=pltpu.VMEM)
    operands = [h_dense]
    if before is not None:
        operands.append(before)
    operands += list(local) + parts
    specs = [pl.BlockSpec(memory_space=pl.ANY)] + [vmem] * len(operands)
    if after is not None:
        operands.append(after)
        specs.append(pl.BlockSpec(memory_space=pl.ANY))
    depth = 256 * sum(g[0] for g in groups)
    scratch = [
        pltpu.VMEM((2 * PACK + BS, 128), BF16),
        pltpu.VMEM((depth, 1024), BF16),
        pltpu.VMEM((256, depth), BF16),
        pltpu.SMEM((32, 64), jnp.int32),
        pltpu.SemaphoreType.DMA,
    ]
    if local:
        scratch += [pltpu.VMEM((256, 1024), BF16), pltpu.VMEM((3, 256, 256), BF16)]
    return pl.pallas_call(
        functools.partial(accumulate_kernel, groups, before is None, bool(local), after is not None),
        out_shape=(jax.ShapeDtypeStruct((256, 1024), F32), jax.ShapeDtypeStruct((8, 128), F32)),
        in_specs=specs,
        out_specs=(vmem, vmem),
        scratch_shapes=scratch,
        compiler_params=pltpu.CompilerParams(vmem_limit_bytes=12 * 2**20),
        cost_estimate=FREE,
    )(table, *operands)


def front(buffer, token):
    anywhere = pl.BlockSpec(memory_space=pl.ANY)
    shape = (2 * PACK, 128)

    def kernel(buffer_ref, token_ref, out_ref, sem):
        copy = pltpu.make_async_copy(buffer_ref.at[pl.ds(0, 2 * PACK), :], out_ref, sem)
        copy.start()
        copy.wait()

    return pl.pallas_call(
        kernel,
        out_shape=jax.ShapeDtypeStruct(shape, buffer.dtype),
        in_specs=[anywhere, anywhere],
        out_specs=anywhere,
        scratch_shapes=[pltpu.SemaphoreType.DMA],
        compiler_params=pltpu.CompilerParams(vmem_limit_bytes=2**20),
        cost_estimate=FREE,
    )(buffer, token)


def hermite(distance):
    scaled = (distance + (0.5 - CUBE / 2.0)) * SCALE
    inside = (distance >= 0) & (distance < CUBE)
    gaussian = jnp.where(inside, jnp.exp(-0.5 * scaled * scaled), 0.0)
    return gaussian, scaled


def powers(distance):
    gaussian, scaled = hermite(distance)
    first = scaled * gaussian
    second = scaled * first
    return gaussian, first, second, scaled * second


def split2(value):
    high = value.astype(BF16)
    return high, (value - high.astype(F32)).astype(BF16)


def three_passes(a, b, dims):
    high, low = split2(a)
    terms = ((high, b[1]), (low, b[0]), (high, b[0]))
    total = None
    for left, right in terms:
        part = lax.dot_general(left, right, dims, preferred_element_type=F32)
        total = part if total is None else total + part
    return total


ROWS = [(a, 2 * bh + bl) for bl in range(2) for a in range(4) for bh in range(2)]


def grid_kernel(info_ref, external_hbm, density_ref, share_ref, gx_ref, gy_ref, gz_ref, u_ref, s_ref, external_ref, sem):
    lanes = 256
    copy = pltpu.make_async_copy(external_hbm, external_ref, sem)
    copy.start()
    cell = lax.broadcasted_iota(jnp.int32, (CUBE, lanes), 0).astype(F32)
    place = lax.broadcasted_iota(jnp.int32, (1, lanes), 1)
    off_x = info_ref[16:17, :] + CUBE * (place // 48 - 1).astype(F32)
    off_y = info_ref[17:18, :] + CUBE * (place % 48 // 16 - 1).astype(F32)
    off_z = info_ref[18:19, :]
    for n, value in enumerate(powers(cell - off_x + CUBE // 2)):
        gx_ref[n] = value
    for n, value in enumerate(powers(cell - off_y + CUBE // 2)):
        gy_ref[n] = value
    deep = lax.broadcasted_iota(jnp.int32, (128, lanes), 0).astype(F32)
    away = deep - off_z + CUBE // 2
    away = jnp.where(away < 0, away + 128.0, away)
    away = jnp.where(away >= 128, away - 128.0, away)
    kinds = powers(away)
    e = lax.broadcasted_iota(jnp.int32, (128, lanes), 1) % 4
    gz_ref[...] = jnp.where(e == 0, kinds[0], jnp.where(e == 1, kinds[1], jnp.where(e == 2, kinds[2], kinds[3])))
    for b in range(4):
        total = None
        for a in range(4):
            at = ROWS.index((a, b))
            term = info_ref[at : at + 1, :] * gx_ref[a]
            total = term if total is None else total + term
        u_ref[b] = total
    s_ref[...] = jnp.zeros_like(s_ref)
    gz = split2(gz_ref[...])
    chunk = 8
    copy.wait()

    def step(i, _):
        planes = []
        x0 = pl.multiple_of(i * chunk, chunk)
        rows_u = [u_ref[b, pl.ds(x0, chunk), :] for b in range(4)]
        rows_g = [gx_ref[a, pl.ds(x0, chunk), :] for a in range(4)]
        for x in range(chunk):
            plane = None
            for b in range(4):
                term = rows_u[b][x : x + 1, :] * gy_ref[b]
                plane = term if plane is None else plane + term
            planes.append(plane)
        spread = jnp.concatenate(planes, axis=0)
        density = three_passes(spread, gz, (((1,), (1,)), ((), ())))
        density = density.reshape(chunk, CUBE, 128)
        density_ref[pl.ds(x0, chunk)] = density
        potential = external_ref[pl.ds(x0, chunk)] + jnp.tanh(density)
        along = three_passes(potential.reshape(chunk * CUBE, 128), gz, (((1,), (0,)), ((), ())))
        for a in range(4):
            total = None
            for x in range(chunk):
                term = along[x * CUBE : (x + 1) * CUBE, :] * rows_g[a][x : x + 1, :]
                total = term if total is None else total + term
            s_ref[a] += total
        return 0

    lax.fori_loop(0, CUBE // chunk, step, 0)
    for at, (a, b) in enumerate(ROWS):
        share_ref[at : at + 1, :] = (
            jnp.sum(s_ref[a] * gy_ref[b], axis=0, keepdims=True) * SCALE**3
        )


def grid_part(info, external):
    vmem = pl.BlockSpec(memory_space=pltpu.VMEM)
    return pl.pallas_call(
        grid_kernel,
        out_shape=(
            jax.ShapeDtypeStruct(external.shape, F32),
            jax.ShapeDtypeStruct((16, 256), F32),
        ),
        in_specs=[vmem, pl.BlockSpec(memory_space=pltpu.HBM)],
        out_specs=(vmem, vmem),
        scratch_shapes=[
            pltpu.VMEM((4, CUBE, 256), F32),
            pltpu.VMEM((4, CUBE, 256), F32),
            pltpu.VMEM((128, 256), F32),
            pltpu.VMEM((4, CUBE, 256), F32),
            pltpu.VMEM((4, CUBE, 256), F32),
            pltpu.VMEM(external.shape, F32),
            pltpu.SemaphoreType.DMA,
        ],
        compiler_params=pltpu.CompilerParams(vmem_limit_bytes=12 * 2**20),
        cost_estimate=FREE,
    )(info, external)


def collect_kernel(near_ref, next_ref, last_ref, far_ref, atoms_ref, mine_ref):
    col = lax.axis_index("col")
    y, x = col // 4, col % 4
    total = jnp.zeros((16, 128), F32)
    for ref, dx in ((near_ref, 0), (next_ref, 1), (last_ref, 3), (far_ref, 2)):
        for j in range(2):
            source = (y + j) % 2 * 4 + (x + dx) % 4
            total += pltpu.roll(ref[16 * j : 16 * j + 16, :], (source + 7) % 8 * 16, 1)
    atoms_ref[...] = total
    mine = pltpu.roll(total, (8 - col) % 8 * 16, 1)
    lane = lax.broadcasted_iota(jnp.int32, (16, 128), 1)
    l = lax.broadcasted_iota(jnp.int32, (128, 64), 0)
    m = lax.broadcasted_iota(jnp.int32, (128, 64), 1)
    move = jnp.where(l % 4 == m % 4, 1.0, 0.0)
    rho = lax.broadcasted_iota(jnp.int32, (16, 64), 0)
    match = lax.broadcasted_iota(jnp.int32, (16, 64), 1) // 4 == rho % 8 // 2 * 4 + rho % 2 * 2 + rho // 8
    for i in range(4):
        value = jnp.dot(
            jnp.where(lane // 4 == i, mine, 0.0), move, precision=PRECISE, preferred_element_type=F32
        )
        mine_ref[i : i + 1, :] = jnp.sum(jnp.where(match, value, 0.0), axis=0, keepdims=True)


def collect(parts):
    vmem = pl.BlockSpec(memory_space=pltpu.VMEM)
    return pl.pallas_call(
        collect_kernel,
        out_shape=(jax.ShapeDtypeStruct((16, 128), F32), jax.ShapeDtypeStruct((4, 64), F32)),
        in_specs=[vmem] * 4,
        out_specs=(vmem, vmem),
        compiler_params=pltpu.CompilerParams(vmem_limit_bytes=2 * 2**20),
        cost_estimate=FREE,
    )(*parts)


def row_of(y, z, core):
    return (y % 2 * 8 + z % 8) * 2 + core % 2


SITES = [(y, z, core) for y in range(2) for z in range(8) for core in range(2)]
ACROSS_Y = [(row_of(*s), row_of(s[0] + 1, s[1], s[2])) for s in SITES]
ACROSS_CORES = [(row_of(*s), row_of(s[0], s[1], s[2] + 1)) for s in SITES]
ALONG_Z = [(row_of(*s), row_of(s[0], s[1] + 1 - 2 * s[2], s[2])) for s in SITES]
COLS = [(y, x) for y in range(2) for x in range(4)]


def col_pairs(dy, dx):
    return [(y * 4 + x, (y + dy) % 2 * 4 + (x + dx) % 4) for y, x in COLS]


ALONG_X = [
    (r * 8 + y * 4 + x, r * 8 + y * 4 + (x + 1 - 2 * (r % 2)) % 4) for r in range(32) for y, x in COLS
]


def ring(axis, size, step):
    return [(i, (i + step) % size) for i in range(size)]


def from_rows(core, last, first):
    mine = jnp.where(core == 0, last, first)
    near = lax.ppermute(mine, "row", ACROSS_CORES)
    mine = jnp.where(core == 0, first, last)
    far = lax.ppermute(mine, "row", [(i, (i + 2 * (i % 2) - 1) % 32) for i in range(32)])
    return jnp.where(core == 0, far, near), jnp.where(core == 0, near, far)


def from_neighbours(last, first, axis, size):
    before = lax.ppermute(last, axis, ring(axis, size, 1))
    after = lax.ppermute(first, axis, ring(axis, size, -1))
    return before, after


def on_device(coefficients, off_x, off_y, off_z, external, pattern, hamiltonian, density_matrix):
    core = lax.axis_index("row") % 2
    hp, pp, info = pack(
        pattern, hamiltonian, density_matrix, coefficients, off_x, off_y, off_z
    )
    table_p, table_h = tile_tables(pattern)

    def step(chain):
        return lax.ppermute(chain, "row", ALONG_Z)

    def swap(chain):
        return lax.ppermute(chain, "row", ACROSS_CORES)

    together = lax.optimization_barrier

    py = lax.ppermute(pp, "row", ACROSS_Y)
    hy = lax.ppermute(hp, "col", col_pairs(1, 0))
    before, after = from_neighbours(info, info, "col", 8)
    info = jnp.concatenate([before, info, after], axis=1)
    pc = swap(pp)
    h0 = jnp.concatenate([hp, hy], axis=0)
    py, pc, info = together((py, pc, info))
    q = jnp.concatenate([pp, py, pc, swap(py)], axis=0)
    q, info = together((q, info))

    q1 = step(q)
    before, after = from_rows(core, info, info)
    info = jnp.concatenate([before, info, after, jnp.zeros((24, 112), F32)], axis=1)
    density, share = grid_part(info, external)
    q1, share, h0 = together((q1, share, h0))

    q2, x1 = step(q1), swap(q1)
    h_next = lax.ppermute(h0, "col", col_pairs(0, 3))
    h_last = lax.ppermute(h0, "col", col_pairs(0, 1))
    before, after = from_rows(core, share[:, 96:144], share[:, 0:48])
    share = share[:, 48:96] + before + after
    share = jnp.concatenate([share, jnp.zeros((16, 80), F32)], axis=1)
    q2, share, h_next, h_last = together((q2, share, h_next, h_last))

    q3, x2 = step(q2), swap(q2)
    h_far = lax.ppermute(jnp.where(core == 0, h_last, h_next), ("row", "col"), ALONG_X)
    h_dense = spread_hamiltonian(table_h, [h0, h_next, h_last, h_far])
    other = lax.ppermute(share, "col", col_pairs(1, 0))
    share = jnp.concatenate([share, other], axis=0)
    product, done = accumulate(
        table_p, h_dense, None, [q, q1, x1], ((4, 0, 0), (4, -1, 0), (4, 1, 1))
    )
    q3, share, product = together((q3, share, product))

    q4 = step(front(q3, done))
    x3 = swap(q3)
    shares = [share] + [lax.ppermute(share, "col", col_pairs(0, d)) for d in (3, 1, 2)]
    product, _ = accumulate(table_p, h_dense, product, [q2, x2], ((4, -2, 0), (4, 2, 1)))
    atoms, integrals = collect(shares)
    q4, atoms, product = together((q4, atoms, product))
    product, _ = accumulate(
        table_p, h_dense, product, [q3, x3], ((4, -3, 0), (4, 3, 1)), local=(atoms, pp)
    )
    product, _ = accumulate(table_p, h_dense, product, [q4, swap(q4)], ((2, 4, 0), (2, 4, 1)))
    return (density, integrals, product)


def solution(mesh):
    return jax.shard_map(
        on_device,
        mesh=mesh,
        in_specs=(
            P(("row", "col"), None),
            P(("row", "col")),
            P(("row", "col")),
            P(("row", "col")),
            P("row", "col", None),
            P(),
            P("row", "col"),
            P("row", "col"),
        ),
        out_specs=(P("row", "col", None), P(("row", "col"), None), P("row", "col")),
        check_vma=False,
    )
```

```python
import functools

import jax
import jax.numpy as jnp
from jax import lax
from jax.experimental import pallas as pl
from jax.experimental.pallas import tpu as pltpu
from jax.sharding import PartitionSpec as P

BS = 64
CUBE = 32
SLOTS = 24
PACK = SLOTS // 2 * BS
F32 = jnp.float32
BF16 = jnp.bfloat16
PRECISE = lax.Precision.HIGHEST
SCALE = 6.0 / CUBE
FREE = pl.CostEstimate(flops=0, bytes_accessed=0, transcendentals=0)


def swap_halves(block):
    return jnp.concatenate([block[:, BS:], block[:, :BS]], axis=1)


def atom_rows(coef_ref, offset_refs, info_ref, wide):
    rho = lax.broadcasted_iota(jnp.int32, (16, 64), 0)
    lane = lax.broadcasted_iota(jnp.int32, (16, 64), 1)
    match = lane // 4 == rho % 8 // 2 * 4 + rho % 2 * 2 + rho // 8
    for i in range(4):
        wide[:, 64 * i : 64 * i + 64] = jnp.where(match, coef_ref[i : i + 1, :], 0.0)
    m = lax.broadcasted_iota(jnp.int32, (256, 128), 0)
    target = lax.broadcasted_iota(jnp.int32, (256, 128), 1)
    move = jnp.where((target // 4 == m // 64) & (target % 4 == m % 4), 1.0, 0.0)
    total = jnp.dot(wide[...], move, precision=PRECISE, preferred_element_type=F32)
    info_ref[0:16, :] = total[:, :16]
    atom = lax.broadcasted_iota(jnp.int32, (8, 16), 1) // 4
    line = lax.broadcasted_iota(jnp.int32, (8, 16), 0)
    lower = jnp.zeros((8, 16), F32)
    for k, ref in enumerate(offset_refs):
        for i in range(4):
            lower = jnp.where((line == k) & (atom == i), ref[i].astype(F32), lower)
    info_ref[16:24, :] = lower


def pack_kernel(
    pattern_hbm, h_hbm, p_hbm, coef_hbm, x_hbm, y_hbm, z_hbm, hp_ref, pp_ref, info_ref,
    rows, places, h_ref, p_ref, coef_ref, x_ref, y_ref, z_ref, wide, sems,
):
    row, col = lax.axis_index("row"), lax.axis_index("col")
    copies = [
        pltpu.make_async_copy(
            pattern_hbm.at[pl.ds(pl.multiple_of(row // 2 * 8, 8), 8), :], rows, sems.at[0]
        ),
        pltpu.make_async_copy(p_hbm, p_ref, sems.at[1]),
        pltpu.make_async_copy(h_hbm, h_ref, sems.at[2]),
        pltpu.make_async_copy(coef_hbm, coef_ref, sems.at[3]),
        pltpu.make_async_copy(x_hbm, x_ref, sems.at[4]),
        pltpu.make_async_copy(y_hbm, y_ref, sems.at[5]),
        pltpu.make_async_copy(z_hbm, z_ref, sems.at[6]),
    ]
    for copy in copies:
        copy.start()

    def clear(i, _):
        places[i] = 0
        return 0

    lax.fori_loop(0, SLOTS + 1, clear, 0)
    copies[0].wait()
    count = jnp.int32(0)
    for block in range(64):
        places[count] = block
        flag = rows[row % 2 * 4 + block // 16, col * 16 + block % 16]
        count = count + jnp.where(flag != 0, 1, 0)
    left = lax.broadcasted_iota(jnp.int32, (BS, 2 * BS), 1) < BS
    for copy, source, target in ((copies[1], p_ref, pp_ref), (copies[2], h_ref, hp_ref)):
        copy.wait()
        for at in range(0, SLOTS // 2, 4):
            blocks = []
            for pair in range(at, at + 4):
                halves = []
                for half in range(2):
                    place = places[2 * pair + half]
                    r, c = place // 16, place % 16
                    block = source[
                        pl.ds(pl.multiple_of(r * BS, BS), BS),
                        pl.ds(pl.multiple_of(c // 2 * 128, 128), 128),
                    ]
                    halves.append(jnp.where(c % 2 == half, block, swap_halves(block)))
                blocks.append(jnp.where(left, halves[0], halves[1]))
            for k, block in enumerate(blocks):
                target[pl.ds((at + k) * BS, BS), :] = block
    for copy in copies[3:]:
        copy.wait()
    atom_rows(coef_ref, (x_ref, y_ref, z_ref), info_ref, wide)


def pack(*operands):
    packed = jax.ShapeDtypeStruct((PACK, 128), BF16)
    vmem = pl.BlockSpec(memory_space=pltpu.VMEM)
    return pl.pallas_call(
        pack_kernel,
        out_shape=(packed, packed, jax.ShapeDtypeStruct((24, 16), F32)),
        in_specs=[pl.BlockSpec(memory_space=pltpu.HBM)] * 7,
        out_specs=(vmem, vmem, vmem),
        scratch_shapes=[
            pltpu.SMEM((8, 128), jnp.int32),
            pltpu.SMEM((SLOTS + 8,), jnp.int32),
            pltpu.VMEM((256, 1024), BF16),
            pltpu.VMEM((256, 1024), BF16),
            pltpu.VMEM((4, 64), F32),
            pltpu.SMEM((4,), jnp.int32),
            pltpu.SMEM((4,), jnp.int32),
            pltpu.SMEM((4,), jnp.int32),
            pltpu.VMEM((16, 256), F32),
            pltpu.SemaphoreType.DMA((7,)),
        ],
        compiler_params=pltpu.CompilerParams(vmem_limit_bytes=58 * 2**20),
        cost_estimate=FREE,
    )(*operands)


def offsets_of(slot, flags):
    slot = slot.astype(jnp.int32)
    parity = lax.broadcasted_iota(jnp.int32, slot.shape, 1) % 2
    at = slot // 2 * BS + jnp.where(slot % 2 == parity, 0, PACK)
    return jnp.where(flags > 0, at, 2 * PACK)


def table_kernel(pattern_ref, p_ref, h_ref, held):
    row, col = lax.axis_index("row"), lax.axis_index("col")
    r = lax.broadcasted_iota(jnp.int32, (128, 128), 0)
    m = lax.broadcasted_iota(jnp.int32, (128, 128), 1)

    def product(a, b):
        return jnp.dot(a.astype(BF16), b.astype(BF16), preferred_element_type=F32)

    def ones(where):
        return jnp.where(where, 1.0, 0.0)

    flags = ones(pattern_ref[...] != 0)
    mine = jnp.where(m < 16, pltpu.roll(flags, (8 - col) % 8 * 16, 1), 0.0)
    above = ones((r // 4 == m // 4) & (m < r))
    slot = product(mine, ones((r < m) & (m < 16)))
    slot += product(above, product(mine, ones(r < 16)))
    held[...] = offsets_of(slot, mine)
    total = jnp.zeros((32, 128), jnp.int32)
    lane = lax.broadcasted_iota(jnp.int32, (32, 128), 1)
    for b in range(4):
        part = jnp.where(lane < 16, held[pl.ds(b, 32, stride=4), :], 0)
        total += pltpu.roll(part, 16 * b, 1) if b else part
    p_ref[...] = total[:, :64]

    two = ones(pattern_ref[pl.ds(pl.multiple_of(row // 2 * 8, 8), 8), :] != 0)
    two = jnp.where(row % 2 == 0, two, pltpu.roll(two, 4, 0))
    four = jnp.where(lax.broadcasted_iota(jnp.int32, (8, 128), 0) < 4, two, 0.0)
    before = product(four, ones((r // 16 == m // 16) & (r < m)))
    whole = product(four, ones(r // 16 == m // 16))
    up = lax.broadcasted_iota(jnp.int32, (8, 8), 1) < lax.broadcasted_iota(jnp.int32, (8, 8), 0)
    before += jnp.dot(ones(up), whole, precision=PRECISE, preferred_element_type=F32)
    h_ref[...] = offsets_of(before, four)


def tile_tables(pattern):
    vmem = pl.BlockSpec(memory_space=pltpu.VMEM)
    return pl.pallas_call(
        table_kernel,
        out_shape=(
            jax.ShapeDtypeStruct((32, 64), jnp.int32),
            jax.ShapeDtypeStruct((8, 128), jnp.int32),
        ),
        in_specs=[vmem],
        out_specs=(vmem, vmem),
        scratch_shapes=[pltpu.VMEM((128, 128), jnp.int32)],
        compiler_params=pltpu.CompilerParams(vmem_limit_bytes=4 * 2**20),
        cost_estimate=FREE,
    )(pattern)


SPAN = 2 * PACK + BS


def prepare(packed, both, base):
    both[pl.ds(base, PACK), :] = packed
    both[pl.ds(base + PACK, PACK), :] = swap_halves(packed)
    both[pl.ds(base + 2 * PACK, BS), :] = jnp.zeros((BS, 128), BF16)


def spread_tile(offset, both, base, store):
    left = lax.broadcasted_iota(jnp.int32, (BS, 2 * BS), 1) < BS
    for r in range(4):
        for first in (0, 4):
            blocks = []
            for c in range(first, first + 4):
                at0 = pl.multiple_of(base + offset(r, 2 * c), BS)
                at1 = pl.multiple_of(base + offset(r, 2 * c + 1), BS)
                blocks.append(jnp.where(left, both[pl.ds(at0, BS), :], both[pl.ds(at1, BS), :]))
            for k, block in enumerate(blocks):
                store(r, first + k, block)


def spread_kernel(table_ref, near_ref, next_ref, last_ref, far_ref, out_ref, both, table, sem):
    copy = pltpu.make_async_copy(table_ref, table, sem)
    copy.start()
    col = lax.axis_index("col")
    y, x = col // 4, col % 4
    parts = ((near_ref, 0), (next_ref, 1), (last_ref, 3), (far_ref, 2))
    for k, (part, _) in enumerate(parts):
        for j in range(2):
            prepare(part[j * PACK : j * PACK + PACK, :], both, (2 * k + j) * SPAN)
    copy.wait()
    for k, (_, dx) in enumerate(parts):

        def one(j, _, k=k, dx=dx):
            source = (y + j) % 2 * 4 + (x + dx) % 4

            def store(r, c, block):
                out_ref[
                    source * 4 + c // 2, r * BS : (r + 1) * BS, c % 2 * 128 : c % 2 * 128 + 128
                ] = block

            base = pl.multiple_of((2 * k + j) * SPAN, BS)
            spread_tile(lambda r, c: table[r, source * 16 + c], both, base, store)
            return 0

        lax.fori_loop(0, 2, one, 0)


def spread_hamiltonian(table, parts):
    vmem = pl.BlockSpec(memory_space=pltpu.VMEM)
    return pl.pallas_call(
        spread_kernel,
        out_shape=jax.ShapeDtypeStruct((32, 256, 256), BF16),
        in_specs=[pl.BlockSpec(memory_space=pl.ANY)] + [vmem] * len(parts),
        out_specs=vmem,
        scratch_shapes=[
            pltpu.VMEM((8 * SPAN, 128), BF16),
            pltpu.SMEM((8, 128), jnp.int32),
            pltpu.SemaphoreType.DMA,
        ],
        compiler_params=pltpu.CompilerParams(vmem_limit_bytes=8 * 2**20),
        cost_estimate=FREE,
    )(table, *parts)


def split3(value):
    high = value.astype(BF16)
    rest = value - high.astype(F32)
    middle = rest.astype(BF16)
    return high, middle, (rest - middle.astype(F32)).astype(BF16)


def tiles_of(groups):
    row = lax.axis_index("row")
    y, z, core = row // 16, row // 2 % 8, row % 2
    direction = 1 - 2 * core
    tiles = []
    for count, steps, flip in groups:
        for j in range(count):
            tiles.append(
                ((y + j) % 2 * 8 + (z + steps * direction + 8) % 8) * 2 + (core + flip + j // 2) % 2
            )
    return tiles


def prepare_all(parts, groups, both):
    at = 0
    for part, (count, _, _) in zip(parts, groups):
        for j in range(count):
            prepare(part[j * PACK : j * PACK + PACK, :], both, at * SPAN)
            at += 1


def spread_all(groups, tiles, table, both, dense, first=0):
    at = 0
    for count, _, _ in groups:

        def one(j, _, at=at, count=count):
            tile = tiles[at]
            for k in range(1, count):
                tile = jnp.where(j == k, tiles[at + k], tile)
            row = pl.multiple_of((first + at + j) * 256, 256)

            def store(r, c, block):
                dense[pl.ds(row + r * BS, BS), c * 128 : c * 128 + 128] = block

            base = pl.multiple_of((at + j) * SPAN, BS)
            spread_tile(lambda r, c: table[tile, r * 16 + c], both, base, store)
            return 0

        lax.fori_loop(0, count, one, 0)
        at += count


def unpack_kernel(groups, table_ref, *refs):
    parts, (dense, both, table, sem) = refs[: len(groups)], refs[len(groups) :]
    copy = pltpu.make_async_copy(table_ref, table, sem)
    copy.start()
    prepare_all(parts, groups, both)
    copy.wait()
    spread_all(groups, tiles_of(groups), table, both, dense)


def unpack(table, parts, groups):
    vmem = pl.BlockSpec(memory_space=pltpu.VMEM)
    count = sum(g[0] for g in groups)
    return pl.pallas_call(
        functools.partial(unpack_kernel, groups),
        out_shape=jax.ShapeDtypeStruct((256 * count, 1024), BF16),
        in_specs=[pl.BlockSpec(memory_space=pl.ANY)] + [vmem] * len(parts),
        out_specs=vmem,
        scratch_shapes=[
            pltpu.VMEM((count * SPAN, 128), BF16),
            pltpu.SMEM((32, 64), jnp.int32),
            pltpu.SemaphoreType.DMA,
        ],
        compiler_params=pltpu.CompilerParams(vmem_limit_bytes=8 * 2**20),
        cost_estimate=FREE,
    )(table, *parts)


def accumulate_kernel(ready, groups, start, local, last, table_ref, h_ref, *refs):
    refs = list(refs)
    before = None if start else refs.pop(0)
    atoms, mine = (refs.pop(0), refs.pop(0)) if local else (None, None)
    early = refs.pop(0) if ready else None
    parts = [refs.pop(0) for _ in groups]
    out_ref, token_ref, both, dense, wide, table, sem = refs[:7]
    copy = pltpu.make_async_copy(table_ref, table, sem)
    copy.start()
    token_ref[...] = jnp.zeros_like(token_ref)
    done, tiles = tiles_of(ready), tiles_of(groups)
    prepare_all(parts, groups, both)
    if local:
        prepare(mine[0:PACK, :], both, len(tiles) * SPAN)
    for at, tile in enumerate(done + tiles):
        wide[:, at * 256 : at * 256 + 256] = h_ref[tile]
    copy.wait()
    spread_all(groups, tiles, table, both, dense)
    if local:
        own, held = refs[7], refs[8]
        row = lax.axis_index("row")

        def store(r, c, block):
            own[r * BS : r * BS + BS, c * 128 : c * 128 + 128] = block

        spread_tile(lambda r, c: table[row, r * 16 + c], both, len(tiles) * SPAN, store)
        values = atoms[...]
        lane_atom = lax.broadcasted_iota(jnp.int32, (256, 128), 1) // 4
        row_atom = lax.broadcasted_iota(jnp.int32, (256, 128), 0) // 8
        tall = [
            jnp.where(
                lane_atom == row_atom,
                jnp.concatenate([values[8 * b : 8 * b + 8, :]] * 32, axis=0),
                0.0,
            )
            for b in range(2)
        ]
        q = lax.broadcasted_iota(jnp.int32, (256, 256), 0)
        m = lax.broadcasted_iota(jnp.int32, (256, 256), 1)
        place = q % 128 // 4 * 8 + q // 128 * 4 + q % 4
        chosen = jnp.where(place == m, 1.0, 0.0).astype(BF16)
        for k, t in enumerate(split3(jnp.concatenate(tall, axis=1))):
            held[k] = jnp.dot(t, chosen, preferred_element_type=F32).astype(BF16)
    copies = []
    for n in range(4):
        lanes = slice(n * 256, n * 256 + 256)
        total = jnp.dot(
            wide[:, len(done) * 256 :], dense[:, lanes], preferred_element_type=F32
        )
        if ready:
            total += jnp.dot(
                wide[:, : len(done) * 256], early[:, lanes], preferred_element_type=F32
            )
        if local:
            for k in range(3):
                total += jnp.dot(held[k], own[:, lanes], preferred_element_type=F32)
        if before is not None:
            total += before[:, lanes]
        if last:
            result, sems = refs[7], refs[8]
            result[:, lanes] = total
            copies.append(
                pltpu.make_async_copy(result.at[:, lanes], out_ref.at[:, lanes], sems.at[n])
            )
            copies[-1].start()
        else:
            out_ref[:, lanes] = total
    for copy in copies:
        copy.wait()


def accumulate(table, h_dense, before, parts, groups, local=(), ready=(), early=None, last=False):
    vmem = pl.BlockSpec(memory_space=pltpu.VMEM)
    operands = [h_dense]
    if before is not None:
        operands.append(before)
    operands += list(local)
    if ready:
        operands.append(early)
    operands += parts
    count = sum(g[0] for g in groups)
    scratch = [
        pltpu.VMEM(((count + bool(local)) * SPAN, 128), BF16),
        pltpu.VMEM((256 * count, 1024), BF16),
        pltpu.VMEM((256, 256 * (count + sum(g[0] for g in ready))), BF16),
        pltpu.SMEM((32, 64), jnp.int32),
        pltpu.SemaphoreType.DMA,
    ]
    if local:
        scratch += [pltpu.VMEM((256, 1024), BF16), pltpu.VMEM((3, 256, 256), BF16)]
    if last:
        scratch += [pltpu.VMEM((256, 1024), F32), pltpu.SemaphoreType.DMA((4,))]
    return pl.pallas_call(
        functools.partial(
            accumulate_kernel, ready, groups, before is None, bool(local), last
        ),
        out_shape=(jax.ShapeDtypeStruct((256, 1024), F32), jax.ShapeDtypeStruct((8, 128), F32)),
        in_specs=[pl.BlockSpec(memory_space=pl.ANY)] + [vmem] * len(operands),
        out_specs=(pl.BlockSpec(memory_space=pltpu.HBM) if last else vmem, vmem),
        scratch_shapes=scratch,
        compiler_params=pltpu.CompilerParams(vmem_limit_bytes=14 * 2**20),
        cost_estimate=FREE,
    )(table, *operands)


def front(buffer, token):
    anywhere = pl.BlockSpec(memory_space=pl.ANY)
    shape = (2 * PACK, 128)

    def kernel(buffer_ref, token_ref, out_ref, sem):
        copy = pltpu.make_async_copy(buffer_ref.at[pl.ds(0, 2 * PACK), :], out_ref, sem)
        copy.start()
        copy.wait()

    return pl.pallas_call(
        kernel,
        out_shape=jax.ShapeDtypeStruct(shape, buffer.dtype),
        in_specs=[anywhere, anywhere],
        out_specs=anywhere,
        scratch_shapes=[pltpu.SemaphoreType.DMA],
        compiler_params=pltpu.CompilerParams(vmem_limit_bytes=2**20),
        cost_estimate=FREE,
    )(buffer, token)


def hermite(distance):
    scaled = (distance + (0.5 - CUBE / 2.0)) * SCALE
    inside = (distance >= 0) & (distance < CUBE)
    gaussian = jnp.where(inside, jnp.exp(-0.5 * scaled * scaled), 0.0)
    return gaussian, scaled


def powers(distance):
    gaussian, scaled = hermite(distance)
    first = scaled * gaussian
    second = scaled * first
    return gaussian, first, second, scaled * second


def split2(value):
    high = value.astype(BF16)
    return high, (value - high.astype(F32)).astype(BF16)


def three_passes(a, b, dims):
    high, low = split2(a)
    terms = ((high, b[1]), (low, b[0]), (high, b[0]))
    total = None
    for left, right in terms:
        part = lax.dot_general(left, right, dims, preferred_element_type=F32)
        total = part if total is None else total + part
    return total


ROWS = [(a, 2 * bh + bl) for bl in range(2) for a in range(4) for bh in range(2)]


def grid_kernel(info_ref, external_hbm, density_ref, own_ref, near_ref, far_ref, gx_ref, gy_ref, gz_ref, u_ref, s_ref, external_ref, held_ref, sem):
    lanes = 256
    copy = pltpu.make_async_copy(external_hbm, external_ref, sem)
    copy.start()
    cell = lax.broadcasted_iota(jnp.int32, (CUBE, lanes), 0).astype(F32)
    place = lax.broadcasted_iota(jnp.int32, (1, lanes), 1)
    turn = 1 - 2 * (lax.axis_index("row") % 2)
    beside = jnp.where(place < 48, 0, jnp.where(place < 96, turn, -turn))
    off_x = info_ref[16:17, :] + CUBE * beside.astype(F32)
    off_y = info_ref[17:18, :] + CUBE * (place % 48 // 16 - 1).astype(F32)
    off_z = info_ref[18:19, :]
    for n, value in enumerate(powers(cell - off_x + CUBE // 2)):
        gx_ref[n] = value
    for n, value in enumerate(powers(cell - off_y + CUBE // 2)):
        gy_ref[n] = value
    deep = lax.broadcasted_iota(jnp.int32, (128, lanes), 0).astype(F32)
    away = deep - off_z + CUBE // 2
    away = jnp.where(away < 0, away + 128.0, away)
    away = jnp.where(away >= 128, away - 128.0, away)
    kinds = powers(away)
    e = lax.broadcasted_iota(jnp.int32, (128, lanes), 1) % 4
    gz_ref[...] = jnp.where(e == 0, kinds[0], jnp.where(e == 1, kinds[1], jnp.where(e == 2, kinds[2], kinds[3])))
    for b in range(4):
        total = None
        for a in range(4):
            at = ROWS.index((a, b))
            term = info_ref[at : at + 1, :] * gx_ref[a]
            total = term if total is None else total + term
        u_ref[b] = total
    s_ref[...] = jnp.zeros_like(s_ref)
    gz = split2(gz_ref[...])
    chunk = 8
    copy.wait()

    def step(i, _):
        planes = []
        x0 = pl.multiple_of(i * chunk, chunk)
        rows_u = [u_ref[b, pl.ds(x0, chunk), :] for b in range(4)]
        rows_g = [gx_ref[a, pl.ds(x0, chunk), :] for a in range(4)]
        for x in range(chunk):
            plane = None
            for b in range(4):
                term = rows_u[b][x : x + 1, :] * gy_ref[b]
                plane = term if plane is None else plane + term
            planes.append(plane)
        spread = jnp.concatenate(planes, axis=0)
        density = three_passes(spread, gz, (((1,), (1,)), ((), ())))
        density = density.reshape(chunk, CUBE, 128)
        density_ref[pl.ds(x0, chunk)] = density
        potential = external_ref[pl.ds(x0, chunk)] + jnp.tanh(density)
        along = three_passes(potential.reshape(chunk * CUBE, 128), gz, (((1,), (0,)), ((), ())))
        for a in range(4):
            total = None
            for x in range(chunk):
                term = along[x * CUBE : (x + 1) * CUBE, :] * rows_g[a][x : x + 1, :]
                total = term if total is None else total + term
            s_ref[a] += total
        return 0

    lax.fori_loop(0, CUBE // chunk, step, 0)
    col = lax.axis_index("col")
    for at, (a, b) in enumerate(ROWS):
        held_ref[at : at + 1, :] = (
            jnp.sum(s_ref[a] * gy_ref[b], axis=0, keepdims=True) * SCALE**3
        )
    share = held_ref[...]
    lane = lax.broadcasted_iota(jnp.int32, (16, 128), 1)
    for k, ref in enumerate((own_ref, near_ref, far_ref)):
        part = share if k == 0 else pltpu.roll(share, lanes - 48 * k, 1)
        ref[...] = pltpu.roll(jnp.where(lane < 48, part[:, :128], 0.0), (col + 7) % 8 * 16, 1)


def grid_part(info, external):
    vmem = pl.BlockSpec(memory_space=pltpu.VMEM)
    return pl.pallas_call(
        grid_kernel,
        out_shape=(
            jax.ShapeDtypeStruct(external.shape, F32),
            *[jax.ShapeDtypeStruct((16, 128), F32)] * 3,
        ),
        in_specs=[vmem, pl.BlockSpec(memory_space=pltpu.HBM)],
        out_specs=(vmem,) * 4,
        scratch_shapes=[
            pltpu.VMEM((4, CUBE, 256), F32),
            pltpu.VMEM((4, CUBE, 256), F32),
            pltpu.VMEM((128, 256), F32),
            pltpu.VMEM((4, CUBE, 256), F32),
            pltpu.VMEM((4, CUBE, 256), F32),
            pltpu.VMEM(external.shape, F32),
            pltpu.VMEM((16, 256), F32),
            pltpu.SemaphoreType.DMA,
        ],
        compiler_params=pltpu.CompilerParams(vmem_limit_bytes=12 * 2**20),
        cost_estimate=FREE,
    )(info, external)


def finish_kernel(atoms_ref, mine_ref):
    col = lax.axis_index("col")
    mine = pltpu.roll(atoms_ref[...], (8 - col) % 8 * 16, 1)
    lane = lax.broadcasted_iota(jnp.int32, (16, 128), 1)
    l = lax.broadcasted_iota(jnp.int32, (128, 64), 0)
    m = lax.broadcasted_iota(jnp.int32, (128, 64), 1)
    move = jnp.where(l % 4 == m % 4, 1.0, 0.0)
    rho = lax.broadcasted_iota(jnp.int32, (16, 64), 0)
    match = lax.broadcasted_iota(jnp.int32, (16, 64), 1) // 4 == rho % 8 // 2 * 4 + rho % 2 * 2 + rho // 8
    parts = jnp.concatenate([jnp.where(lane // 4 == i, mine, 0.0) for i in range(4)], axis=0)
    values = jnp.dot(parts, move, precision=PRECISE, preferred_element_type=F32)
    for i in range(4):
        value = jnp.where(match, values[16 * i : 16 * i + 16, :], 0.0)
        mine_ref[i : i + 1, :] = jnp.sum(value, axis=0, keepdims=True)


def finish(atoms):
    vmem = pl.BlockSpec(memory_space=pltpu.VMEM)
    return pl.pallas_call(
        finish_kernel,
        out_shape=jax.ShapeDtypeStruct((4, 64), F32),
        in_specs=[vmem],
        out_specs=vmem,
        compiler_params=pltpu.CompilerParams(vmem_limit_bytes=2 * 2**20),
        cost_estimate=FREE,
    )(atoms)


def row_of(y, z, core):
    return (y % 2 * 8 + z % 8) * 2 + core % 2


SITES = [(y, z, core) for y in range(2) for z in range(8) for core in range(2)]
ACROSS_Y = [(row_of(*s), row_of(s[0] + 1, s[1], s[2])) for s in SITES]
ACROSS_CORES = [(row_of(*s), row_of(s[0], s[1], s[2] + 1)) for s in SITES]
ALONG_Z = [(row_of(*s), row_of(s[0], s[1] + 1 - 2 * s[2], s[2])) for s in SITES]
COLS = [(y, x) for y in range(2) for x in range(4)]


def col_pairs(dy, dx):
    return [(y * 4 + x, (y + dy) % 2 * 4 + (x + dx) % 4) for y, x in COLS]


ALONG_X = [
    (r * 8 + y * 4 + x, r * 8 + y * 4 + (x + 1 - 2 * (r % 2)) % 4) for r in range(32) for y, x in COLS
]


def ring(axis, size, step):
    return [(i, (i + step) % size) for i in range(size)]


def to_rows(near, far):
    near = lax.ppermute(near, "row", ACROSS_CORES)
    return near, lax.ppermute(far, "row", [(i, (i + 2 * (i % 2) - 1) % 32) for i in range(32)])


def from_neighbours(last, first, axis, size):
    before = lax.ppermute(last, axis, ring(axis, size, 1))
    after = lax.ppermute(first, axis, ring(axis, size, -1))
    return before, after


def on_device(coefficients, off_x, off_y, off_z, external, pattern, hamiltonian, density_matrix):
    core = lax.axis_index("row") % 2
    hp, pp, info = pack(
        pattern, hamiltonian, density_matrix, coefficients, off_x, off_y, off_z
    )
    table_p, table_h = tile_tables(pattern)

    def step(chain):
        return lax.ppermute(chain, "row", ALONG_Z)

    def swap(chain):
        return lax.ppermute(chain, "row", ACROSS_CORES)

    together = lax.optimization_barrier

    py = lax.ppermute(pp, "row", ACROSS_Y)
    hy = lax.ppermute(hp, "col", col_pairs(1, 0))
    before, after = from_neighbours(info, info, "col", 8)
    info = jnp.concatenate([before, info, after], axis=1)
    pc = swap(pp)
    near, far = to_rows(info, info)
    py, pc, info, hy, table_p, table_h = together((py, pc, info, hy, table_p, table_h))
    info = jnp.concatenate([info, near, far, jnp.zeros((24, 112), F32)], axis=1)
    q = jnp.concatenate([pp, py, pc, swap(py)], axis=0)
    q, info = together((q, info))
    h0 = jnp.concatenate([hp, hy], axis=0)

    q1 = step(q)
    h_next = lax.ppermute(h0, "col", col_pairs(0, 3))
    h_last = lax.ppermute(h0, "col", col_pairs(0, 1))
    density, share, near, far = grid_part(info, external)
    near, far = to_rows(near, far)
    share = share + near + far
    q1, share, h_next, h_last = together((q1, share, h_next, h_last))

    q2, x1 = step(q1), swap(q1)
    h_far = lax.ppermute(jnp.where(core == 0, h_last, h_next), ("row", "col"), ALONG_X)
    share = share + lax.ppermute(share, "col", col_pairs(1, 0))
    share = share + lax.ppermute(share, "col", [(i, i ^ 1) for i in range(8)])
    early_groups = ((4, 0, 0), (4, -1, 0))
    dense = unpack(table_p, [q, q1], early_groups)
    q2, dense, share, h_far = together((q2, dense, share, h_far))
    h_dense = spread_hamiltonian(table_h, [h0, h_next, h_last, h_far])

    q3, x2 = step(q2), swap(q2)
    atoms = share + lax.ppermute(share, "col", [(i, i ^ 2) for i in range(8)])
    product, done = accumulate(
        table_p, h_dense, None, [x1], ((4, 1, 1),), ready=early_groups, early=dense
    )
    q3, atoms, done = together((q3, atoms, done))

    q4 = step(front(q3, done))
    x3 = swap(q3)
    integrals = finish(atoms)
    product, _ = accumulate(table_p, h_dense, product, [q2, x2], ((4, -2, 0), (4, 2, 1)))
    product, _ = accumulate(
        table_p, h_dense, product, [q3, x3], ((4, -3, 0), (4, 3, 1)), local=(atoms, pp)
    )
    q4, product = together((q4, product))
    product, _ = accumulate(table_p, h_dense, product, [q4, swap(q4)], ((2, 4, 0), (2, 4, 1)))
    return (density, integrals, product)


def solution(mesh):
    return jax.shard_map(
        on_device,
        mesh=mesh,
        in_specs=(
            P(("row", "col"), None),
            P(("row", "col")),
            P(("row", "col")),
            P(("row", "col")),
            P("row", "col", None),
            P(),
            P("row", "col"),
            P("row", "col"),
        ),
        out_specs=(P("row", "col", None), P(("row", "col"), None), P("row", "col")),
        check_vma=False,
    )
```

```python
import functools

import jax
import jax.numpy as jnp
from jax import lax
from jax.experimental import pallas as pl
from jax.experimental.pallas import tpu as pltpu
from jax.sharding import PartitionSpec as P

BS = 64
CUBE = 32
SLOTS = 24
PACK = SLOTS // 2 * BS
F32 = jnp.float32
BF16 = jnp.bfloat16
PRECISE = lax.Precision.HIGHEST
SCALE = 6.0 / CUBE
FREE = pl.CostEstimate(flops=0, bytes_accessed=0, transcendentals=0)


def swap_halves(block):
    return jnp.concatenate([block[:, BS:], block[:, :BS]], axis=1)


def atom_rows(coef_ref, offset_refs, info_ref, wide):
    rho = lax.broadcasted_iota(jnp.int32, (16, 64), 0)
    lane = lax.broadcasted_iota(jnp.int32, (16, 64), 1)
    match = lane // 4 == rho % 8 // 2 * 4 + rho % 2 * 2 + rho // 8
    for i in range(4):
        wide[:, 64 * i : 64 * i + 64] = jnp.where(match, coef_ref[i : i + 1, :], 0.0)
    m = lax.broadcasted_iota(jnp.int32, (256, 128), 0)
    target = lax.broadcasted_iota(jnp.int32, (256, 128), 1)
    move = jnp.where((target // 4 == m // 64) & (target % 4 == m % 4), 1.0, 0.0)
    total = jnp.dot(wide[...], move, precision=PRECISE, preferred_element_type=F32)
    info_ref[0:16, :] = total[:, :16]
    atom = lax.broadcasted_iota(jnp.int32, (8, 16), 1) // 4
    line = lax.broadcasted_iota(jnp.int32, (8, 16), 0)
    lower = jnp.zeros((8, 16), F32)
    for k, ref in enumerate(offset_refs):
        for i in range(4):
            lower = jnp.where((line == k) & (atom == i), ref[i].astype(F32), lower)
    info_ref[16:24, :] = lower


def pack_kernel(
    pattern_hbm, h_hbm, p_hbm, coef_hbm, x_hbm, y_hbm, z_hbm, hp_ref, pp_ref, info_ref,
    rows, places, h_ref, p_ref, coef_ref, x_ref, y_ref, z_ref, wide, sems,
):
    row, col = lax.axis_index("row"), lax.axis_index("col")
    copies = [
        pltpu.make_async_copy(
            pattern_hbm.at[pl.ds(pl.multiple_of(row // 2 * 8, 8), 8), :], rows, sems.at[0]
        ),
        pltpu.make_async_copy(p_hbm, p_ref, sems.at[1]),
        pltpu.make_async_copy(h_hbm, h_ref, sems.at[2]),
        pltpu.make_async_copy(coef_hbm, coef_ref, sems.at[3]),
        pltpu.make_async_copy(x_hbm, x_ref, sems.at[4]),
        pltpu.make_async_copy(y_hbm, y_ref, sems.at[5]),
        pltpu.make_async_copy(z_hbm, z_ref, sems.at[6]),
    ]
    for copy in copies:
        copy.start()

    def clear(i, _):
        places[i] = 0
        return 0

    lax.fori_loop(0, SLOTS + 1, clear, 0)
    copies[0].wait()
    count = jnp.int32(0)
    for block in range(64):
        places[count] = block
        flag = rows[row % 2 * 4 + block // 16, col * 16 + block % 16]
        count = count + jnp.where(flag != 0, 1, 0)
    left = lax.broadcasted_iota(jnp.int32, (BS, 2 * BS), 1) < BS
    for copy, source, target in ((copies[1], p_ref, pp_ref), (copies[2], h_ref, hp_ref)):
        copy.wait()
        for at in range(0, SLOTS // 2, 4):
            blocks = []
            for pair in range(at, at + 4):
                halves = []
                for half in range(2):
                    place = places[2 * pair + half]
                    r, c = place // 16, place % 16
                    block = source[
                        pl.ds(pl.multiple_of(r * BS, BS), BS),
                        pl.ds(pl.multiple_of(c // 2 * 128, 128), 128),
                    ]
                    halves.append(jnp.where(c % 2 == half, block, swap_halves(block)))
                blocks.append(jnp.where(left, halves[0], halves[1]))
            for k, block in enumerate(blocks):
                target[pl.ds((at + k) * BS, BS), :] = block
    for copy in copies[3:]:
        copy.wait()
    atom_rows(coef_ref, (x_ref, y_ref, z_ref), info_ref, wide)


def pack(*operands):
    packed = jax.ShapeDtypeStruct((PACK, 128), BF16)
    vmem = pl.BlockSpec(memory_space=pltpu.VMEM)
    return pl.pallas_call(
        pack_kernel,
        out_shape=(packed, packed, jax.ShapeDtypeStruct((24, 16), F32)),
        in_specs=[pl.BlockSpec(memory_space=pltpu.HBM)] * 7,
        out_specs=(vmem, vmem, vmem),
        scratch_shapes=[
            pltpu.SMEM((8, 128), jnp.int32),
            pltpu.SMEM((SLOTS + 8,), jnp.int32),
            pltpu.VMEM((256, 1024), BF16),
            pltpu.VMEM((256, 1024), BF16),
            pltpu.VMEM((4, 64), F32),
            pltpu.SMEM((4,), jnp.int32),
            pltpu.SMEM((4,), jnp.int32),
            pltpu.SMEM((4,), jnp.int32),
            pltpu.VMEM((16, 256), F32),
            pltpu.SemaphoreType.DMA((7,)),
        ],
        compiler_params=pltpu.CompilerParams(vmem_limit_bytes=58 * 2**20),
        cost_estimate=FREE,
    )(*operands)


def offsets_of(slot, flags):
    slot = slot.astype(jnp.int32)
    parity = lax.broadcasted_iota(jnp.int32, slot.shape, 1) % 2
    at = slot // 2 * BS + jnp.where(slot % 2 == parity, 0, PACK)
    return jnp.where(flags > 0, at, 2 * PACK)


def table_kernel(pattern_ref, p_ref, h_ref, held):
    row, col = lax.axis_index("row"), lax.axis_index("col")
    r = lax.broadcasted_iota(jnp.int32, (128, 128), 0)
    m = lax.broadcasted_iota(jnp.int32, (128, 128), 1)

    def product(a, b):
        return jnp.dot(a.astype(BF16), b.astype(BF16), preferred_element_type=F32)

    def ones(where):
        return jnp.where(where, 1.0, 0.0)

    flags = ones(pattern_ref[...] != 0)
    mine = jnp.where(m < 16, pltpu.roll(flags, (8 - col) % 8 * 16, 1), 0.0)
    above = ones((r // 4 == m // 4) & (m < r))
    slot = product(mine, ones((r < m) & (m < 16)))
    slot += product(above, product(mine, ones(r < 16)))
    held[...] = offsets_of(slot, mine)
    total = jnp.zeros((32, 128), jnp.int32)
    lane = lax.broadcasted_iota(jnp.int32, (32, 128), 1)
    for b in range(4):
        part = jnp.where(lane < 16, held[pl.ds(b, 32, stride=4), :], 0)
        total += pltpu.roll(part, 16 * b, 1) if b else part
    p_ref[...] = total[:, :64]

    two = ones(pattern_ref[pl.ds(pl.multiple_of(row // 2 * 8, 8), 8), :] != 0)
    two = jnp.where(row % 2 == 0, two, pltpu.roll(two, 4, 0))
    four = jnp.where(lax.broadcasted_iota(jnp.int32, (8, 128), 0) < 4, two, 0.0)
    before = product(four, ones((r // 16 == m // 16) & (r < m)))
    whole = product(four, ones(r // 16 == m // 16))
    up = lax.broadcasted_iota(jnp.int32, (8, 8), 1) < lax.broadcasted_iota(jnp.int32, (8, 8), 0)
    before += jnp.dot(ones(up), whole, precision=PRECISE, preferred_element_type=F32)
    h_ref[...] = offsets_of(before, four)


def tile_tables(pattern):
    vmem = pl.BlockSpec(memory_space=pltpu.VMEM)
    return pl.pallas_call(
        table_kernel,
        out_shape=(
            jax.ShapeDtypeStruct((32, 64), jnp.int32),
            jax.ShapeDtypeStruct((8, 128), jnp.int32),
        ),
        in_specs=[vmem],
        out_specs=(vmem, vmem),
        scratch_shapes=[pltpu.VMEM((128, 128), jnp.int32)],
        compiler_params=pltpu.CompilerParams(vmem_limit_bytes=4 * 2**20),
        cost_estimate=FREE,
    )(pattern)


SPAN = 2 * PACK + BS


def prepare(packed, both, base):
    both[pl.ds(base, PACK), :] = packed
    both[pl.ds(base + PACK, PACK), :] = swap_halves(packed)
    both[pl.ds(base + 2 * PACK, BS), :] = jnp.zeros((BS, 128), BF16)


def spread_tile(offset, both, base, store):
    left = lax.broadcasted_iota(jnp.int32, (BS, 2 * BS), 1) < BS
    for r in range(4):
        for first in (0, 4):
            blocks = []
            for c in range(first, first + 4):
                at0 = pl.multiple_of(base + offset(r, 2 * c), BS)
                at1 = pl.multiple_of(base + offset(r, 2 * c + 1), BS)
                blocks.append(jnp.where(left, both[pl.ds(at0, BS), :], both[pl.ds(at1, BS), :]))
            for k, block in enumerate(blocks):
                store(r, first + k, block)


def spread_kernel(table_ref, near_ref, next_ref, last_ref, far_ref, out_ref, both, table, sem):
    copy = pltpu.make_async_copy(table_ref, table, sem)
    copy.start()
    col = lax.axis_index("col")
    y, x = col // 4, col % 4
    parts = ((near_ref, 0), (next_ref, 1), (last_ref, 3), (far_ref, 2))
    for k, (part, _) in enumerate(parts):
        for j in range(2):
            prepare(part[j * PACK : j * PACK + PACK, :], both, (2 * k + j) * SPAN)
    copy.wait()
    for k, (_, dx) in enumerate(parts):

        def one(j, _, k=k, dx=dx):
            source = (y + j) % 2 * 4 + (x + dx) % 4

            def store(r, c, block):
                out_ref[
                    source * 4 + c // 2, r * BS : (r + 1) * BS, c % 2 * 128 : c % 2 * 128 + 128
                ] = block

            base = pl.multiple_of((2 * k + j) * SPAN, BS)
            spread_tile(lambda r, c: table[r, source * 16 + c], both, base, store)
            return 0

        lax.fori_loop(0, 2, one, 0)


def spread_hamiltonian(table, parts):
    vmem = pl.BlockSpec(memory_space=pltpu.VMEM)
    return pl.pallas_call(
        spread_kernel,
        out_shape=jax.ShapeDtypeStruct((32, 256, 256), BF16),
        in_specs=[pl.BlockSpec(memory_space=pl.ANY)] + [vmem] * len(parts),
        out_specs=vmem,
        scratch_shapes=[
            pltpu.VMEM((8 * SPAN, 128), BF16),
            pltpu.SMEM((8, 128), jnp.int32),
            pltpu.SemaphoreType.DMA,
        ],
        compiler_params=pltpu.CompilerParams(vmem_limit_bytes=8 * 2**20),
        cost_estimate=FREE,
    )(table, *parts)


def split3(value):
    high = value.astype(BF16)
    rest = value - high.astype(F32)
    middle = rest.astype(BF16)
    return high, middle, (rest - middle.astype(F32)).astype(BF16)


def tiles_of(groups):
    row = lax.axis_index("row")
    y, z, core = row // 16, row // 2 % 8, row % 2
    direction = 1 - 2 * core
    tiles = []
    for count, steps, flip in groups:
        for j in range(count):
            tiles.append(
                ((y + j) % 2 * 8 + (z + steps * direction + 8) % 8) * 2 + (core + flip + j // 2) % 2
            )
    return tiles


def prepare_all(parts, groups, both):
    at = 0
    for part, (count, _, _) in zip(parts, groups):
        for j in range(count):
            prepare(part[j * PACK : j * PACK + PACK, :], both, at * SPAN)
            at += 1


def spread_all(groups, tiles, table, both, dense, first=0):
    at = 0
    for count, _, _ in groups:

        def one(j, _, at=at, count=count):
            tile = tiles[at]
            for k in range(1, count):
                tile = jnp.where(j == k, tiles[at + k], tile)
            row = pl.multiple_of((first + at + j) * 256, 256)

            def store(r, c, block):
                dense[pl.ds(row + r * BS, BS), c * 128 : c * 128 + 128] = block

            base = pl.multiple_of((at + j) * SPAN, BS)
            spread_tile(lambda r, c: table[tile, r * 16 + c], both, base, store)
            return 0

        lax.fori_loop(0, count, one, 0)
        at += count


def unpack_kernel(groups, table_ref, *refs):
    parts, (dense, both, table, sem) = refs[: len(groups)], refs[len(groups) :]
    copy = pltpu.make_async_copy(table_ref, table, sem)
    copy.start()
    prepare_all(parts, groups, both)
    copy.wait()
    spread_all(groups, tiles_of(groups), table, both, dense)


def unpack(table, parts, groups):
    vmem = pl.BlockSpec(memory_space=pltpu.VMEM)
    count = sum(g[0] for g in groups)
    return pl.pallas_call(
        functools.partial(unpack_kernel, groups),
        out_shape=jax.ShapeDtypeStruct((256 * count, 1024), BF16),
        in_specs=[pl.BlockSpec(memory_space=pl.ANY)] + [vmem] * len(parts),
        out_specs=vmem,
        scratch_shapes=[
            pltpu.VMEM((count * SPAN, 128), BF16),
            pltpu.SMEM((32, 64), jnp.int32),
            pltpu.SemaphoreType.DMA,
        ],
        compiler_params=pltpu.CompilerParams(vmem_limit_bytes=8 * 2**20),
        cost_estimate=FREE,
    )(table, *parts)


def accumulate_kernel(ready, groups, start, local, table_ref, h_ref, *refs):
    refs = list(refs)
    before = None if start else refs.pop(0)
    held, own = (refs.pop(0), refs.pop(0)) if local else (None, None)
    early = refs.pop(0) if ready else None
    parts = [refs.pop(0) for _ in groups]
    out_ref, token_ref, both, dense, wide, table, sem = refs[:7]
    copy = pltpu.make_async_copy(table_ref, table, sem)
    copy.start()
    token_ref[...] = jnp.zeros_like(token_ref)
    done, tiles = tiles_of(ready), tiles_of(groups)
    prepare_all(parts, groups, both)
    for at, tile in enumerate(done + tiles):
        wide[:, at * 256 : at * 256 + 256] = h_ref[tile]
    copy.wait()
    spread_all(groups, tiles, table, both, dense)
    for n in range(4):
        lanes = slice(n * 256, n * 256 + 256)
        total = jnp.dot(
            wide[:, len(done) * 256 :], dense[:, lanes], preferred_element_type=F32
        )
        if ready:
            total += jnp.dot(
                wide[:, : len(done) * 256], early[:, lanes], preferred_element_type=F32
            )
        if local:
            for k in range(3):
                total += jnp.dot(held[k], own[0:256, lanes], preferred_element_type=F32)
        if before is not None:
            total += before[:, lanes]
        out_ref[:, lanes] = total


def accumulate(table, h_dense, before, parts, groups, local=(), ready=(), early=None):
    vmem = pl.BlockSpec(memory_space=pltpu.VMEM)
    operands = [h_dense]
    if before is not None:
        operands.append(before)
    operands += list(local)
    if ready:
        operands.append(early)
    operands += parts
    count = sum(g[0] for g in groups)
    scratch = [
        pltpu.VMEM((count * SPAN, 128), BF16),
        pltpu.VMEM((256 * count, 1024), BF16),
        pltpu.VMEM((256, 256 * (count + sum(g[0] for g in ready))), BF16),
        pltpu.SMEM((32, 64), jnp.int32),
        pltpu.SemaphoreType.DMA,
    ]
    return pl.pallas_call(
        functools.partial(accumulate_kernel, ready, groups, before is None, bool(local)),
        out_shape=(jax.ShapeDtypeStruct((256, 1024), F32), jax.ShapeDtypeStruct((8, 128), F32)),
        in_specs=[pl.BlockSpec(memory_space=pl.ANY)] + [vmem] * len(operands),
        out_specs=(vmem, vmem),
        scratch_shapes=scratch,
        compiler_params=pltpu.CompilerParams(vmem_limit_bytes=14 * 2**20),
        cost_estimate=FREE,
    )(table, *operands)


def front(buffer, token):
    anywhere = pl.BlockSpec(memory_space=pl.ANY)
    shape = (2 * PACK, 128)

    def kernel(buffer_ref, token_ref, out_ref, sem):
        copy = pltpu.make_async_copy(buffer_ref.at[pl.ds(0, 2 * PACK), :], out_ref, sem)
        copy.start()
        copy.wait()

    return pl.pallas_call(
        kernel,
        out_shape=jax.ShapeDtypeStruct(shape, buffer.dtype),
        in_specs=[anywhere, anywhere],
        out_specs=anywhere,
        scratch_shapes=[pltpu.SemaphoreType.DMA],
        compiler_params=pltpu.CompilerParams(vmem_limit_bytes=2**20),
        cost_estimate=FREE,
    )(buffer, token)


def hermite(distance):
    scaled = (distance + (0.5 - CUBE / 2.0)) * SCALE
    inside = (distance >= 0) & (distance < CUBE)
    gaussian = jnp.where(inside, jnp.exp(-0.5 * scaled * scaled), 0.0)
    return gaussian, scaled


def powers(distance):
    gaussian, scaled = hermite(distance)
    first = scaled * gaussian
    second = scaled * first
    return gaussian, first, second, scaled * second


def split2(value):
    high = value.astype(BF16)
    return high, (value - high.astype(F32)).astype(BF16)


def three_passes(a, b, dims):
    high, low = split2(a)
    terms = ((high, b[1]), (low, b[0]), (high, b[0]))
    total = None
    for left, right in terms:
        part = lax.dot_general(left, right, dims, preferred_element_type=F32)
        total = part if total is None else total + part
    return total


ROWS = [(a, 2 * bh + bl) for bl in range(2) for a in range(4) for bh in range(2)]


def grid_kernel(info_ref, external_hbm, density_ref, own_ref, near_ref, far_ref, gx_ref, gy_ref, gz_ref, u_ref, s_ref, external_ref, held_ref, sem):
    lanes = 256
    copy = pltpu.make_async_copy(external_hbm, external_ref, sem)
    copy.start()
    cell = lax.broadcasted_iota(jnp.int32, (CUBE, lanes), 0).astype(F32)
    place = lax.broadcasted_iota(jnp.int32, (1, lanes), 1)
    turn = 1 - 2 * (lax.axis_index("row") % 2)
    beside = jnp.where(place < 48, 0, jnp.where(place < 96, turn, -turn))
    off_x = info_ref[16:17, :] + CUBE * beside.astype(F32)
    off_y = info_ref[17:18, :] + CUBE * (place % 48 // 16 - 1).astype(F32)
    off_z = info_ref[18:19, :]
    for n, value in enumerate(powers(cell - off_x + CUBE // 2)):
        gx_ref[n] = value
    for n, value in enumerate(powers(cell - off_y + CUBE // 2)):
        gy_ref[n] = value
    deep = lax.broadcasted_iota(jnp.int32, (128, lanes), 0).astype(F32)
    away = deep - off_z + CUBE // 2
    away = jnp.where(away < 0, away + 128.0, away)
    away = jnp.where(away >= 128, away - 128.0, away)
    kinds = powers(away)
    e = lax.broadcasted_iota(jnp.int32, (128, lanes), 1) % 4
    gz_ref[...] = jnp.where(e == 0, kinds[0], jnp.where(e == 1, kinds[1], jnp.where(e == 2, kinds[2], kinds[3])))
    for b in range(4):
        total = None
        for a in range(4):
            at = ROWS.index((a, b))
            term = info_ref[at : at + 1, :] * gx_ref[a]
            total = term if total is None else total + term
        u_ref[b] = total
    s_ref[...] = jnp.zeros_like(s_ref)
    gz = split2(gz_ref[...])
    chunk = 8
    copy.wait()

    def step(i, _):
        planes = []
        x0 = pl.multiple_of(i * chunk, chunk)
        rows_u = [u_ref[b, pl.ds(x0, chunk), :] for b in range(4)]
        rows_g = [gx_ref[a, pl.ds(x0, chunk), :] for a in range(4)]
        for x in range(chunk):
            plane = None
            for b in range(4):
                term = rows_u[b][x : x + 1, :] * gy_ref[b]
                plane = term if plane is None else plane + term
            planes.append(plane)
        spread = jnp.concatenate(planes, axis=0)
        density = three_passes(spread, gz, (((1,), (1,)), ((), ())))
        density = density.reshape(chunk, CUBE, 128)
        density_ref[pl.ds(x0, chunk)] = density
        potential = external_ref[pl.ds(x0, chunk)] + jnp.tanh(density)
        along = three_passes(potential.reshape(chunk * CUBE, 128), gz, (((1,), (0,)), ((), ())))
        for a in range(4):
            total = None
            for x in range(chunk):
                term = along[x * CUBE : (x + 1) * CUBE, :] * rows_g[a][x : x + 1, :]
                total = term if total is None else total + term
            s_ref[a] += total
        return 0

    lax.fori_loop(0, CUBE // chunk, step, 0)
    col = lax.axis_index("col")
    for at, (a, b) in enumerate(ROWS):
        held_ref[at : at + 1, :] = (
            jnp.sum(s_ref[a] * gy_ref[b], axis=0, keepdims=True) * SCALE**3
        )
    share = held_ref[...]
    lane = lax.broadcasted_iota(jnp.int32, (16, 128), 1)
    for k, ref in enumerate((own_ref, near_ref, far_ref)):
        part = share if k == 0 else pltpu.roll(share, lanes - 48 * k, 1)
        ref[...] = pltpu.roll(jnp.where(lane < 48, part[:, :128], 0.0), (col + 7) % 8 * 16, 1)


def grid_part(info, external):
    vmem = pl.BlockSpec(memory_space=pltpu.VMEM)
    return pl.pallas_call(
        grid_kernel,
        out_shape=(
            jax.ShapeDtypeStruct(external.shape, F32),
            *[jax.ShapeDtypeStruct((16, 128), F32)] * 3,
        ),
        in_specs=[vmem, pl.BlockSpec(memory_space=pltpu.HBM)],
        out_specs=(vmem,) * 4,
        scratch_shapes=[
            pltpu.VMEM((4, CUBE, 256), F32),
            pltpu.VMEM((4, CUBE, 256), F32),
            pltpu.VMEM((128, 256), F32),
            pltpu.VMEM((4, CUBE, 256), F32),
            pltpu.VMEM((4, CUBE, 256), F32),
            pltpu.VMEM(external.shape, F32),
            pltpu.VMEM((16, 256), F32),
            pltpu.SemaphoreType.DMA,
        ],
        compiler_params=pltpu.CompilerParams(vmem_limit_bytes=12 * 2**20),
        cost_estimate=FREE,
    )(info, external)


def finish_kernel(atoms_ref, mine_ref, terms_ref):
    values = atoms_ref[...]
    lane_atom = lax.broadcasted_iota(jnp.int32, (256, 128), 1) // 4
    row_atom = lax.broadcasted_iota(jnp.int32, (256, 128), 0) // 8
    tall = [
        jnp.where(
            lane_atom == row_atom,
            jnp.concatenate([values[8 * b : 8 * b + 8, :]] * 32, axis=0),
            0.0,
        )
        for b in range(2)
    ]
    q = lax.broadcasted_iota(jnp.int32, (256, 256), 0)
    m = lax.broadcasted_iota(jnp.int32, (256, 256), 1)
    place = q % 128 // 4 * 8 + q // 128 * 4 + q % 4
    chosen = jnp.where(place == m, 1.0, 0.0).astype(BF16)
    for k, t in enumerate(split3(jnp.concatenate(tall, axis=1))):
        terms_ref[k] = jnp.dot(t, chosen, preferred_element_type=F32).astype(BF16)
    col = lax.axis_index("col")
    mine = pltpu.roll(atoms_ref[...], (8 - col) % 8 * 16, 1)
    lane = lax.broadcasted_iota(jnp.int32, (16, 128), 1)
    l = lax.broadcasted_iota(jnp.int32, (128, 64), 0)
    m = lax.broadcasted_iota(jnp.int32, (128, 64), 1)
    move = jnp.where(l % 4 == m % 4, 1.0, 0.0)
    rho = lax.broadcasted_iota(jnp.int32, (16, 64), 0)
    match = lax.broadcasted_iota(jnp.int32, (16, 64), 1) // 4 == rho % 8 // 2 * 4 + rho % 2 * 2 + rho // 8
    parts = jnp.concatenate([jnp.where(lane // 4 == i, mine, 0.0) for i in range(4)], axis=0)
    values = jnp.dot(parts, move, precision=PRECISE, preferred_element_type=F32)
    for i in range(4):
        value = jnp.where(match, values[16 * i : 16 * i + 16, :], 0.0)
        mine_ref[i : i + 1, :] = jnp.sum(value, axis=0, keepdims=True)


def finish(atoms):
    vmem = pl.BlockSpec(memory_space=pltpu.VMEM)
    return pl.pallas_call(
        finish_kernel,
        out_shape=(
            jax.ShapeDtypeStruct((4, 64), F32),
            jax.ShapeDtypeStruct((3, 256, 256), BF16),
        ),
        in_specs=[vmem],
        out_specs=(vmem, vmem),
        compiler_params=pltpu.CompilerParams(vmem_limit_bytes=2 * 2**20),
        cost_estimate=FREE,
    )(atoms)


def row_of(y, z, core):
    return (y % 2 * 8 + z % 8) * 2 + core % 2


SITES = [(y, z, core) for y in range(2) for z in range(8) for core in range(2)]
ACROSS_Y = [(row_of(*s), row_of(s[0] + 1, s[1], s[2])) for s in SITES]
ACROSS_CORES = [(row_of(*s), row_of(s[0], s[1], s[2] + 1)) for s in SITES]
ALONG_Z = [(row_of(*s), row_of(s[0], s[1] + 1 - 2 * s[2], s[2])) for s in SITES]
COLS = [(y, x) for y in range(2) for x in range(4)]


def col_pairs(dy, dx):
    return [(y * 4 + x, (y + dy) % 2 * 4 + (x + dx) % 4) for y, x in COLS]


ALONG_X = [
    (r * 8 + y * 4 + x, r * 8 + y * 4 + (x + 1 - 2 * (r % 2)) % 4) for r in range(32) for y, x in COLS
]


def ring(axis, size, step):
    return [(i, (i + step) % size) for i in range(size)]


def to_rows(near, far):
    near = lax.ppermute(near, "row", ACROSS_CORES)
    return near, lax.ppermute(far, "row", [(i, (i + 2 * (i % 2) - 1) % 32) for i in range(32)])


def from_neighbours(last, first, axis, size):
    before = lax.ppermute(last, axis, ring(axis, size, 1))
    after = lax.ppermute(first, axis, ring(axis, size, -1))
    return before, after


def on_device(coefficients, off_x, off_y, off_z, external, pattern, hamiltonian, density_matrix):
    core = lax.axis_index("row") % 2
    hp, pp, info = pack(
        pattern, hamiltonian, density_matrix, coefficients, off_x, off_y, off_z
    )
    table_p, table_h = tile_tables(pattern)

    def step(chain):
        return lax.ppermute(chain, "row", ALONG_Z)

    def swap(chain):
        return lax.ppermute(chain, "row", ACROSS_CORES)

    together = lax.optimization_barrier

    py = lax.ppermute(pp, "row", ACROSS_Y)
    hy = lax.ppermute(hp, "col", col_pairs(1, 0))
    before, after = from_neighbours(info, info, "col", 8)
    info = jnp.concatenate([before, info, after], axis=1)
    pc = swap(pp)
    near, far = to_rows(info, info)
    py, pc, info, hy, table_p, table_h = together((py, pc, info, hy, table_p, table_h))
    info = jnp.concatenate([info, near, far, jnp.zeros((24, 112), F32)], axis=1)
    q = jnp.concatenate([pp, py, pc, swap(py)], axis=0)
    q, info = together((q, info))
    h0 = jnp.concatenate([hp, hy], axis=0)

    q1 = step(q)
    h_next = lax.ppermute(h0, "col", col_pairs(0, 3))
    h_last = lax.ppermute(h0, "col", col_pairs(0, 1))
    density, share, near, far = grid_part(info, external)
    near, far = to_rows(near, far)
    share = share + near + far
    q1, share = together((q1, share))

    q2, x1 = step(q1), swap(q1)
    h_far = lax.ppermute(jnp.where(core == 0, h_last, h_next), ("row", "col"), ALONG_X)
    share, h_next, h_last = together((share, h_next, h_last))
    share = share + lax.ppermute(share, "col", col_pairs(1, 0))
    early_groups = ((4, 0, 0), (4, -1, 0))
    dense = unpack(table_p, [q, q1], early_groups)
    share, dense = together((share, dense))
    share = share + lax.ppermute(share, "col", [(i, i ^ 1) for i in range(8)])
    q2, dense, share, h_far = together((q2, dense, share, h_far))
    h_dense = spread_hamiltonian(table_h, [h0, h_next, h_last, h_far])

    q3, x2 = step(q2), swap(q2)
    atoms = share + lax.ppermute(share, "col", [(i, i ^ 2) for i in range(8)])
    product, done = accumulate(
        table_p, h_dense, None, [x1], ((4, 1, 1),), ready=early_groups, early=dense
    )
    integrals, terms = finish(atoms)
    dense2 = unpack(table_p, [q2], ((4, -2, 0),))
    q3, integrals, terms, dense2, done = together((q3, integrals, terms, dense2, done))

    q4 = step(front(q3, done))
    x3 = swap(q3)
    product, _ = accumulate(
        table_p, h_dense, product, [x2], ((4, 2, 1),), ready=((4, -2, 0),), early=dense2
    )
    product, _ = accumulate(
        table_p, h_dense, product, [q3, x3], ((4, -3, 0), (4, 3, 1)), local=(terms, dense)
    )
    q4, product = together((q4, product))
    x4 = swap(q4)
    dense4 = unpack(table_p, [q4], ((2, 4, 0),))
    product, _ = accumulate(
        table_p, h_dense, product, [x4], ((2, 4, 1),), ready=((2, 4, 0),), early=dense4
    )
    return (density, integrals, product)


def solution(mesh):
    return jax.shard_map(
        on_device,
        mesh=mesh,
        in_specs=(
            P(("row", "col"), None),
            P(("row", "col")),
            P(("row", "col")),
            P(("row", "col")),
            P("row", "col", None),
            P(),
            P("row", "col"),
            P("row", "col"),
        ),
        out_specs=(P("row", "col", None), P(("row", "col"), None), P("row", "col")),
        check_vma=False,
    )
```

```python
import functools

import jax
import jax.numpy as jnp
from jax import lax
from jax.experimental import pallas as pl
from jax.experimental.pallas import tpu as pltpu
from jax.sharding import PartitionSpec as P

BS = 64
CUBE = 32
SLOTS = 24
PACK = SLOTS // 2 * BS
F32 = jnp.float32
BF16 = jnp.bfloat16
PRECISE = lax.Precision.HIGHEST
SCALE = 6.0 / CUBE
FREE = pl.CostEstimate(flops=0, bytes_accessed=0, transcendentals=0)


def swap_halves(block):
    return jnp.concatenate([block[:, BS:], block[:, :BS]], axis=1)


def atom_rows(coef_ref, offset_refs, info_ref, wide):
    rho = lax.broadcasted_iota(jnp.int32, (16, 64), 0)
    lane = lax.broadcasted_iota(jnp.int32, (16, 64), 1)
    match = lane // 4 == rho % 8 // 2 * 4 + rho % 2 * 2 + rho // 8
    for i in range(4):
        wide[:, 64 * i : 64 * i + 64] = jnp.where(match, coef_ref[i : i + 1, :], 0.0)
    m = lax.broadcasted_iota(jnp.int32, (256, 128), 0)
    target = lax.broadcasted_iota(jnp.int32, (256, 128), 1)
    move = jnp.where((target // 4 == m // 64) & (target % 4 == m % 4), 1.0, 0.0)
    total = jnp.dot(wide[...], move, precision=PRECISE, preferred_element_type=F32)
    info_ref[0:16, :] = total[:, :16]
    atom = lax.broadcasted_iota(jnp.int32, (8, 16), 1) // 4
    line = lax.broadcasted_iota(jnp.int32, (8, 16), 0)
    lower = jnp.zeros((8, 16), F32)
    for k, ref in enumerate(offset_refs):
        for i in range(4):
            lower = jnp.where((line == k) & (atom == i), ref[i].astype(F32), lower)
    info_ref[16:24, :] = lower


def pack_kernel(
    pattern_hbm, h_hbm, p_hbm, coef_hbm, x_hbm, y_hbm, z_hbm, hp_ref, pp_ref, info_ref,
    rows, places, h_ref, p_ref, coef_ref, x_ref, y_ref, z_ref, wide, sems,
):
    row, col = lax.axis_index("row"), lax.axis_index("col")
    copies = [
        pltpu.make_async_copy(
            pattern_hbm.at[pl.ds(pl.multiple_of(row // 2 * 8, 8), 8), :], rows, sems.at[0]
        ),
        pltpu.make_async_copy(p_hbm, p_ref, sems.at[1]),
        pltpu.make_async_copy(h_hbm, h_ref, sems.at[2]),
        pltpu.make_async_copy(coef_hbm, coef_ref, sems.at[3]),
        pltpu.make_async_copy(x_hbm, x_ref, sems.at[4]),
        pltpu.make_async_copy(y_hbm, y_ref, sems.at[5]),
        pltpu.make_async_copy(z_hbm, z_ref, sems.at[6]),
    ]
    for copy in copies:
        copy.start()

    def clear(i, _):
        places[i] = 0
        return 0

    lax.fori_loop(0, SLOTS + 1, clear, 0)
    copies[0].wait()
    count = jnp.int32(0)
    for block in range(64):
        places[count] = block
        flag = rows[row % 2 * 4 + block // 16, col * 16 + block % 16]
        count = count + jnp.where(flag != 0, 1, 0)
    left = lax.broadcasted_iota(jnp.int32, (BS, 2 * BS), 1) < BS
    for copy, source, target in ((copies[1], p_ref, pp_ref), (copies[2], h_ref, hp_ref)):
        copy.wait()
        for at in range(0, SLOTS // 2, 4):
            blocks = []
            for pair in range(at, at + 4):
                halves = []
                for half in range(2):
                    place = places[2 * pair + half]
                    r, c = place // 16, place % 16
                    block = source[
                        pl.ds(pl.multiple_of(r * BS, BS), BS),
                        pl.ds(pl.multiple_of(c // 2 * 128, 128), 128),
                    ]
                    halves.append(jnp.where(c % 2 == half, block, swap_halves(block)))
                blocks.append(jnp.where(left, halves[0], halves[1]))
            for k, block in enumerate(blocks):
                target[pl.ds((at + k) * BS, BS), :] = block
    for copy in copies[3:]:
        copy.wait()
    atom_rows(coef_ref, (x_ref, y_ref, z_ref), info_ref, wide)


def pack(*operands):
    packed = jax.ShapeDtypeStruct((PACK, 128), BF16)
    vmem = pl.BlockSpec(memory_space=pltpu.VMEM)
    return pl.pallas_call(
        pack_kernel,
        out_shape=(packed, packed, jax.ShapeDtypeStruct((24, 16), F32)),
        in_specs=[pl.BlockSpec(memory_space=pltpu.HBM)] * 7,
        out_specs=(vmem, vmem, vmem),
        scratch_shapes=[
            pltpu.SMEM((8, 128), jnp.int32),
            pltpu.SMEM((SLOTS + 8,), jnp.int32),
            pltpu.VMEM((256, 1024), BF16),
            pltpu.VMEM((256, 1024), BF16),
            pltpu.VMEM((4, 64), F32),
            pltpu.SMEM((4,), jnp.int32),
            pltpu.SMEM((4,), jnp.int32),
            pltpu.SMEM((4,), jnp.int32),
            pltpu.VMEM((16, 256), F32),
            pltpu.SemaphoreType.DMA((7,)),
        ],
        compiler_params=pltpu.CompilerParams(vmem_limit_bytes=58 * 2**20),
        cost_estimate=FREE,
    )(*operands)


def offsets_of(slot, flags):
    slot = slot.astype(jnp.int32)
    parity = lax.broadcasted_iota(jnp.int32, slot.shape, 1) % 2
    at = slot // 2 * BS + jnp.where(slot % 2 == parity, 0, PACK)
    return jnp.where(flags > 0, at, 2 * PACK)


def table_kernel(pattern_ref, p_ref, h_ref, held):
    row, col = lax.axis_index("row"), lax.axis_index("col")
    r = lax.broadcasted_iota(jnp.int32, (128, 128), 0)
    m = lax.broadcasted_iota(jnp.int32, (128, 128), 1)

    def product(a, b):
        return jnp.dot(a.astype(BF16), b.astype(BF16), preferred_element_type=F32)

    def ones(where):
        return jnp.where(where, 1.0, 0.0)

    flags = ones(pattern_ref[...] != 0)
    mine = jnp.where(m < 16, pltpu.roll(flags, (8 - col) % 8 * 16, 1), 0.0)
    above = ones((r // 4 == m // 4) & (m < r))
    slot = product(mine, ones((r < m) & (m < 16)))
    slot += product(above, product(mine, ones(r < 16)))
    held[...] = offsets_of(slot, mine)
    total = jnp.zeros((32, 128), jnp.int32)
    lane = lax.broadcasted_iota(jnp.int32, (32, 128), 1)
    for b in range(4):
        part = jnp.where(lane < 16, held[pl.ds(b, 32, stride=4), :], 0)
        total += pltpu.roll(part, 16 * b, 1) if b else part
    p_ref[...] = total[:, :64]

    two = ones(pattern_ref[pl.ds(pl.multiple_of(row // 2 * 8, 8), 8), :] != 0)
    two = jnp.where(row % 2 == 0, two, pltpu.roll(two, 4, 0))
    four = jnp.where(lax.broadcasted_iota(jnp.int32, (8, 128), 0) < 4, two, 0.0)
    before = product(four, ones((r // 16 == m // 16) & (r < m)))
    whole = product(four, ones(r // 16 == m // 16))
    up = lax.broadcasted_iota(jnp.int32, (8, 8), 1) < lax.broadcasted_iota(jnp.int32, (8, 8), 0)
    before += jnp.dot(ones(up), whole, precision=PRECISE, preferred_element_type=F32)
    h_ref[...] = offsets_of(before, four)


def tile_tables(pattern):
    vmem = pl.BlockSpec(memory_space=pltpu.VMEM)
    return pl.pallas_call(
        table_kernel,
        out_shape=(
            jax.ShapeDtypeStruct((32, 64), jnp.int32),
            jax.ShapeDtypeStruct((8, 128), jnp.int32),
        ),
        in_specs=[vmem],
        out_specs=(vmem, vmem),
        scratch_shapes=[pltpu.VMEM((128, 128), jnp.int32)],
        compiler_params=pltpu.CompilerParams(vmem_limit_bytes=4 * 2**20),
        cost_estimate=FREE,
    )(pattern)


SPAN = 2 * PACK + BS


def prepare(packed, both, base):
    both[pl.ds(base, PACK), :] = packed
    both[pl.ds(base + PACK, PACK), :] = swap_halves(packed)
    both[pl.ds(base + 2 * PACK, BS), :] = jnp.zeros((BS, 128), BF16)


def spread_tile(offset, both, base, store):
    left = lax.broadcasted_iota(jnp.int32, (BS, 2 * BS), 1) < BS
    for r in range(4):
        for first in (0, 4):
            blocks = []
            for c in range(first, first + 4):
                at0 = pl.multiple_of(base + offset(r, 2 * c), BS)
                at1 = pl.multiple_of(base + offset(r, 2 * c + 1), BS)
                blocks.append(jnp.where(left, both[pl.ds(at0, BS), :], both[pl.ds(at1, BS), :]))
            for k, block in enumerate(blocks):
                store(r, first + k, block)


def spread_kernel(table_ref, near_ref, next_ref, last_ref, far_ref, out_ref, both, table, sem):
    copy = pltpu.make_async_copy(table_ref, table, sem)
    copy.start()
    col = lax.axis_index("col")
    y, x = col // 4, col % 4
    parts = ((near_ref, 0), (next_ref, 1), (last_ref, 3), (far_ref, 2))
    for k, (part, _) in enumerate(parts):
        for j in range(2):
            prepare(part[j * PACK : j * PACK + PACK, :], both, (2 * k + j) * SPAN)
    copy.wait()
    for k, (_, dx) in enumerate(parts):

        def one(j, _, k=k, dx=dx):
            source = (y + j) % 2 * 4 + (x + dx) % 4

            def store(r, c, block):
                out_ref[
                    source * 4 + c // 2, r * BS : (r + 1) * BS, c % 2 * 128 : c % 2 * 128 + 128
                ] = block

            base = pl.multiple_of((2 * k + j) * SPAN, BS)
            spread_tile(lambda r, c: table[r, source * 16 + c], both, base, store)
            return 0

        lax.fori_loop(0, 2, one, 0)


def spread_hamiltonian(table, parts):
    vmem = pl.BlockSpec(memory_space=pltpu.VMEM)
    return pl.pallas_call(
        spread_kernel,
        out_shape=jax.ShapeDtypeStruct((32, 256, 256), BF16),
        in_specs=[pl.BlockSpec(memory_space=pl.ANY)] + [vmem] * len(parts),
        out_specs=vmem,
        scratch_shapes=[
            pltpu.VMEM((8 * SPAN, 128), BF16),
            pltpu.SMEM((8, 128), jnp.int32),
            pltpu.SemaphoreType.DMA,
        ],
        compiler_params=pltpu.CompilerParams(vmem_limit_bytes=8 * 2**20),
        cost_estimate=FREE,
    )(table, *parts)


def split3(value):
    high = value.astype(BF16)
    rest = value - high.astype(F32)
    middle = rest.astype(BF16)
    return high, middle, (rest - middle.astype(F32)).astype(BF16)


def tiles_of(groups):
    row = lax.axis_index("row")
    y, z, core = row // 16, row // 2 % 8, row % 2
    direction = 1 - 2 * core
    tiles = []
    for count, steps, flip in groups:
        for j in range(count):
            tiles.append(
                ((y + j) % 2 * 8 + (z + steps * direction + 8) % 8) * 2 + (core + flip + j // 2) % 2
            )
    return tiles


def prepare_all(parts, groups, both):
    at = 0
    for part, (count, _, _) in zip(parts, groups):
        for j in range(count):
            prepare(part[j * PACK : j * PACK + PACK, :], both, at * SPAN)
            at += 1


def spread_all(groups, tiles, table, both, dense, first=0):
    at = 0
    for count, _, _ in groups:

        def one(j, _, at=at, count=count):
            tile = tiles[at]
            for k in range(1, count):
                tile = jnp.where(j == k, tiles[at + k], tile)
            row = pl.multiple_of((first + at + j) * 256, 256)

            def store(r, c, block):
                dense[pl.ds(row + r * BS, BS), c * 128 : c * 128 + 128] = block

            base = pl.multiple_of((at + j) * SPAN, BS)
            spread_tile(lambda r, c: table[tile, r * 16 + c], both, base, store)
            return 0

        lax.fori_loop(0, count, one, 0)
        at += count


def unpack_kernel(groups, table_ref, *refs):
    parts, (dense, both, table, sem) = refs[: len(groups)], refs[len(groups) :]
    copy = pltpu.make_async_copy(table_ref, table, sem)
    copy.start()
    prepare_all(parts, groups, both)
    copy.wait()
    spread_all(groups, tiles_of(groups), table, both, dense)


def unpack(table, parts, groups):
    vmem = pl.BlockSpec(memory_space=pltpu.VMEM)
    count = sum(g[0] for g in groups)
    return pl.pallas_call(
        functools.partial(unpack_kernel, groups),
        out_shape=jax.ShapeDtypeStruct((256 * count, 1024), BF16),
        in_specs=[pl.BlockSpec(memory_space=pl.ANY)] + [vmem] * len(parts),
        out_specs=vmem,
        scratch_shapes=[
            pltpu.VMEM((count * SPAN, 128), BF16),
            pltpu.SMEM((32, 64), jnp.int32),
            pltpu.SemaphoreType.DMA,
        ],
        compiler_params=pltpu.CompilerParams(vmem_limit_bytes=8 * 2**20),
        cost_estimate=FREE,
    )(table, *parts)


def accumulate_kernel(ready, groups, start, local, table_ref, h_ref, *refs):
    refs = list(refs)
    before = None if start else refs.pop(0)
    held, own = (refs.pop(0), refs.pop(0)) if local else (None, None)
    early = refs.pop(0) if ready else None
    parts = [refs.pop(0) for _ in groups]
    out_ref, token_ref, both, dense, wide, table, sem = refs[:7]
    copy = pltpu.make_async_copy(table_ref, table, sem)
    copy.start()
    token_ref[...] = jnp.zeros_like(token_ref)
    done, tiles = tiles_of(ready), tiles_of(groups)
    prepare_all(parts, groups, both)
    for at, tile in enumerate(done + tiles):
        wide[:, at * 256 : at * 256 + 256] = h_ref[tile]
    copy.wait()
    spread_all(groups, tiles, table, both, dense)
    for n in range(4):
        lanes = slice(n * 256, n * 256 + 256)
        total = jnp.dot(
            wide[:, len(done) * 256 :], dense[:, lanes], preferred_element_type=F32
        )
        if ready:
            total += jnp.dot(
                wide[:, : len(done) * 256], early[:, lanes], preferred_element_type=F32
            )
        if local:
            for k in range(3):
                total += jnp.dot(held[k], own[0:256, lanes], preferred_element_type=F32)
        if before is not None:
            total += before[:, lanes]
        out_ref[:, lanes] = total


def accumulate(table, h_dense, before, parts, groups, local=(), ready=(), early=None):
    vmem = pl.BlockSpec(memory_space=pltpu.VMEM)
    operands = [h_dense]
    if before is not None:
        operands.append(before)
    operands += list(local)
    if ready:
        operands.append(early)
    operands += parts
    count = sum(g[0] for g in groups)
    scratch = [
        pltpu.VMEM((count * SPAN, 128), BF16),
        pltpu.VMEM((256 * count, 1024), BF16),
        pltpu.VMEM((256, 256 * (count + sum(g[0] for g in ready))), BF16),
        pltpu.SMEM((32, 64), jnp.int32),
        pltpu.SemaphoreType.DMA,
    ]
    return pl.pallas_call(
        functools.partial(accumulate_kernel, ready, groups, before is None, bool(local)),
        out_shape=(jax.ShapeDtypeStruct((256, 1024), F32), jax.ShapeDtypeStruct((8, 128), F32)),
        in_specs=[pl.BlockSpec(memory_space=pl.ANY)] + [vmem] * len(operands),
        out_specs=(vmem, vmem),
        scratch_shapes=scratch,
        compiler_params=pltpu.CompilerParams(vmem_limit_bytes=14 * 2**20),
        cost_estimate=FREE,
    )(table, *operands)


def front(buffer, token):
    anywhere = pl.BlockSpec(memory_space=pl.ANY)
    shape = (2 * PACK, 128)

    def kernel(buffer_ref, token_ref, out_ref, sem):
        copy = pltpu.make_async_copy(buffer_ref.at[pl.ds(0, 2 * PACK), :], out_ref, sem)
        copy.start()
        copy.wait()

    return pl.pallas_call(
        kernel,
        out_shape=jax.ShapeDtypeStruct(shape, buffer.dtype),
        in_specs=[anywhere, anywhere],
        out_specs=anywhere,
        scratch_shapes=[pltpu.SemaphoreType.DMA],
        compiler_params=pltpu.CompilerParams(vmem_limit_bytes=2**20),
        cost_estimate=FREE,
    )(buffer, token)


def hermite(distance):
    scaled = (distance + (0.5 - CUBE / 2.0)) * SCALE
    inside = (distance >= 0) & (distance < CUBE)
    gaussian = jnp.where(inside, jnp.exp(-0.5 * scaled * scaled), 0.0)
    return gaussian, scaled


def powers(distance):
    gaussian, scaled = hermite(distance)
    first = scaled * gaussian
    second = scaled * first
    return gaussian, first, second, scaled * second


def split2(value):
    high = value.astype(BF16)
    return high, (value - high.astype(F32)).astype(BF16)


def three_passes(a, b, dims):
    high, low = split2(a)
    terms = ((high, b[1]), (low, b[0]), (high, b[0]))
    total = None
    for left, right in terms:
        part = lax.dot_general(left, right, dims, preferred_element_type=F32)
        total = part if total is None else total + part
    return total


ROWS = [(a, 2 * bh + bl) for bl in range(2) for a in range(4) for bh in range(2)]


def grid_kernel(info_ref, external_hbm, density_ref, own_ref, near_ref, far_ref, gx_ref, gy_ref, gz_ref, u_ref, s_ref, external_ref, held_ref, sem):
    lanes = 256
    copy = pltpu.make_async_copy(external_hbm, external_ref, sem)
    copy.start()
    cell = lax.broadcasted_iota(jnp.int32, (CUBE, lanes), 0).astype(F32)
    place = lax.broadcasted_iota(jnp.int32, (1, lanes), 1)
    turn = 1 - 2 * (lax.axis_index("row") % 2)
    beside = jnp.where(place < 48, 0, jnp.where(place < 96, turn, -turn))
    off_x = info_ref[16:17, :] + CUBE * beside.astype(F32)
    off_y = info_ref[17:18, :] + CUBE * (place % 48 // 16 - 1).astype(F32)
    off_z = info_ref[18:19, :]
    for n, value in enumerate(powers(cell - off_x + CUBE // 2)):
        gx_ref[n] = value
    for n, value in enumerate(powers(cell - off_y + CUBE // 2)):
        gy_ref[n] = value
    deep = lax.broadcasted_iota(jnp.int32, (128, lanes), 0).astype(F32)
    away = deep - off_z + CUBE // 2
    away = jnp.where(away < 0, away + 128.0, away)
    away = jnp.where(away >= 128, away - 128.0, away)
    kinds = powers(away)
    e = lax.broadcasted_iota(jnp.int32, (128, lanes), 1) % 4
    gz_ref[...] = jnp.where(e == 0, kinds[0], jnp.where(e == 1, kinds[1], jnp.where(e == 2, kinds[2], kinds[3])))
    for b in range(4):
        total = None
        for a in range(4):
            at = ROWS.index((a, b))
            term = info_ref[at : at + 1, :] * gx_ref[a]
            total = term if total is None else total + term
        u_ref[b] = total
    s_ref[...] = jnp.zeros_like(s_ref)
    gz = split2(gz_ref[...])
    chunk = 8
    copy.wait()

    def step(i, _):
        planes = []
        x0 = pl.multiple_of(i * chunk, chunk)
        rows_u = [u_ref[b, pl.ds(x0, chunk), :] for b in range(4)]
        rows_g = [gx_ref[a, pl.ds(x0, chunk), :] for a in range(4)]
        for x in range(chunk):
            plane = None
            for b in range(4):
                term = rows_u[b][x : x + 1, :] * gy_ref[b]
                plane = term if plane is None else plane + term
            planes.append(plane)
        spread = jnp.concatenate(planes, axis=0)
        density = three_passes(spread, gz, (((1,), (1,)), ((), ())))
        density = density.reshape(chunk, CUBE, 128)
        density_ref[pl.ds(x0, chunk)] = density
        potential = external_ref[pl.ds(x0, chunk)] + jnp.tanh(density)
        along = three_passes(potential.reshape(chunk * CUBE, 128), gz, (((1,), (0,)), ((), ())))
        for a in range(4):
            total = None
            for x in range(chunk):
                term = along[x * CUBE : (x + 1) * CUBE, :] * rows_g[a][x : x + 1, :]
                total = term if total is None else total + term
            s_ref[a] += total
        return 0

    lax.fori_loop(0, CUBE // chunk, step, 0)
    col = lax.axis_index("col")
    for at, (a, b) in enumerate(ROWS):
        held_ref[at : at + 1, :] = (
            jnp.sum(s_ref[a] * gy_ref[b], axis=0, keepdims=True) * SCALE**3
        )
    share = held_ref[...]
    lane = lax.broadcasted_iota(jnp.int32, (16, 128), 1)
    for k, ref in enumerate((own_ref, near_ref, far_ref)):
        part = share if k == 0 else pltpu.roll(share, lanes - 48 * k, 1)
        ref[...] = pltpu.roll(jnp.where(lane < 48, part[:, :128], 0.0), (col + 7) % 8 * 16, 1)


def grid_part(info, external):
    vmem = pl.BlockSpec(memory_space=pltpu.VMEM)
    return pl.pallas_call(
        grid_kernel,
        out_shape=(
            jax.ShapeDtypeStruct(external.shape, F32),
            *[jax.ShapeDtypeStruct((16, 128), F32)] * 3,
        ),
        in_specs=[vmem, pl.BlockSpec(memory_space=pltpu.HBM)],
        out_specs=(vmem,) * 4,
        scratch_shapes=[
            pltpu.VMEM((4, CUBE, 256), F32),
            pltpu.VMEM((4, CUBE, 256), F32),
            pltpu.VMEM((128, 256), F32),
            pltpu.VMEM((4, CUBE, 256), F32),
            pltpu.VMEM((4, CUBE, 256), F32),
            pltpu.VMEM(external.shape, F32),
            pltpu.VMEM((16, 256), F32),
            pltpu.SemaphoreType.DMA,
        ],
        compiler_params=pltpu.CompilerParams(vmem_limit_bytes=12 * 2**20),
        cost_estimate=FREE,
    )(info, external)


def finish_kernel(atoms_ref, mine_ref, terms_ref):
    values = atoms_ref[...]
    lane_atom = lax.broadcasted_iota(jnp.int32, (256, 128), 1) // 4
    row_atom = lax.broadcasted_iota(jnp.int32, (256, 128), 0) // 8
    tall = [
        jnp.where(
            lane_atom == row_atom,
            jnp.concatenate([values[8 * b : 8 * b + 8, :]] * 32, axis=0),
            0.0,
        )
        for b in range(2)
    ]
    q = lax.broadcasted_iota(jnp.int32, (256, 256), 0)
    m = lax.broadcasted_iota(jnp.int32, (256, 256), 1)
    place = q % 128 // 4 * 8 + q // 128 * 4 + q % 4
    chosen = jnp.where(place == m, 1.0, 0.0).astype(BF16)
    for k, t in enumerate(split3(jnp.concatenate(tall, axis=1))):
        terms_ref[k] = jnp.dot(t, chosen, preferred_element_type=F32).astype(BF16)
    col = lax.axis_index("col")
    mine = pltpu.roll(atoms_ref[...], (8 - col) % 8 * 16, 1)
    lane = lax.broadcasted_iota(jnp.int32, (16, 128), 1)
    l = lax.broadcasted_iota(jnp.int32, (128, 64), 0)
    m = lax.broadcasted_iota(jnp.int32, (128, 64), 1)
    move = jnp.where(l % 4 == m % 4, 1.0, 0.0)
    rho = lax.broadcasted_iota(jnp.int32, (16, 64), 0)
    match = lax.broadcasted_iota(jnp.int32, (16, 64), 1) // 4 == rho % 8 // 2 * 4 + rho % 2 * 2 + rho // 8
    parts = jnp.concatenate([jnp.where(lane // 4 == i, mine, 0.0) for i in range(4)], axis=0)
    values = jnp.dot(parts, move, precision=PRECISE, preferred_element_type=F32)
    for i in range(4):
        value = jnp.where(match, values[16 * i : 16 * i + 16, :], 0.0)
        mine_ref[i : i + 1, :] = jnp.sum(value, axis=0, keepdims=True)


def finish(atoms):
    vmem = pl.BlockSpec(memory_space=pltpu.VMEM)
    return pl.pallas_call(
        finish_kernel,
        out_shape=(
            jax.ShapeDtypeStruct((4, 64), F32),
            jax.ShapeDtypeStruct((3, 256, 256), BF16),
        ),
        in_specs=[vmem],
        out_specs=(vmem, vmem),
        compiler_params=pltpu.CompilerParams(vmem_limit_bytes=2 * 2**20),
        cost_estimate=FREE,
    )(atoms)


def row_of(y, z, core):
    return (y % 2 * 8 + z % 8) * 2 + core % 2


SITES = [(y, z, core) for y in range(2) for z in range(8) for core in range(2)]
ACROSS_Y = [(row_of(*s), row_of(s[0] + 1, s[1], s[2])) for s in SITES]
ACROSS_CORES = [(row_of(*s), row_of(s[0], s[1], s[2] + 1)) for s in SITES]
ALONG_Z = [(row_of(*s), row_of(s[0], s[1] + 1 - 2 * s[2], s[2])) for s in SITES]
COLS = [(y, x) for y in range(2) for x in range(4)]


def col_pairs(dy, dx):
    return [(y * 4 + x, (y + dy) % 2 * 4 + (x + dx) % 4) for y, x in COLS]


ALONG_X = [
    (r * 8 + y * 4 + x, r * 8 + y * 4 + (x + 1 - 2 * (r % 2)) % 4) for r in range(32) for y, x in COLS
]


def ring(axis, size, step):
    return [(i, (i + step) % size) for i in range(size)]


def to_rows(near, far):
    near = lax.ppermute(near, "row", ACROSS_CORES)
    return near, lax.ppermute(far, "row", [(i, (i + 2 * (i % 2) - 1) % 32) for i in range(32)])


def from_neighbours(last, first, axis, size):
    before = lax.ppermute(last, axis, ring(axis, size, 1))
    after = lax.ppermute(first, axis, ring(axis, size, -1))
    return before, after


def on_device(coefficients, off_x, off_y, off_z, external, pattern, hamiltonian, density_matrix):
    core = lax.axis_index("row") % 2
    hp, pp, info = pack(
        pattern, hamiltonian, density_matrix, coefficients, off_x, off_y, off_z
    )
    table_p, table_h = tile_tables(pattern)

    def step(chain):
        return lax.ppermute(chain, "row", ALONG_Z)

    def swap(chain):
        return lax.ppermute(chain, "row", ACROSS_CORES)

    together = lax.optimization_barrier

    py = lax.ppermute(pp, "row", ACROSS_Y)
    hy = lax.ppermute(hp, "col", col_pairs(1, 0))
    before, after = from_neighbours(info, info, "col", 8)
    info = jnp.concatenate([before, info, after], axis=1)
    pc = swap(pp)
    near, far = to_rows(info, info)
    py, pc, info, hy = together((py, pc, info, hy))
    info = jnp.concatenate([info, near, far, jnp.zeros((24, 112), F32)], axis=1)
    q = jnp.concatenate([pp, py, pc, swap(py)], axis=0)
    q, info = together((q, info))
    h0 = jnp.concatenate([hp, hy], axis=0)

    q1 = step(q)
    h_next = lax.ppermute(h0, "col", col_pairs(0, 3))
    h_last = lax.ppermute(h0, "col", col_pairs(0, 1))
    density, share, near, far = grid_part(info, external)
    near, far = to_rows(near, far)
    share = share + near + far
    q1, share, table_p, table_h = together((q1, share, table_p, table_h))

    q2, x1 = step(q1), swap(q1)
    h_far = lax.ppermute(jnp.where(core == 0, h_last, h_next), ("row", "col"), ALONG_X)
    share, h_next, h_last = together((share, h_next, h_last))
    share = share + lax.ppermute(share, "col", col_pairs(1, 0))
    early_groups = ((4, 0, 0), (4, -1, 0))
    dense = unpack(table_p, [q, q1], early_groups)
    share, dense = together((share, dense))
    share = share + lax.ppermute(share, "col", [(i, i ^ 1) for i in range(8)])
    q2, dense, share, h_far = together((q2, dense, share, h_far))
    h_dense = spread_hamiltonian(table_h, [h0, h_next, h_last, h_far])

    q3, x2 = step(q2), swap(q2)
    atoms = share + lax.ppermute(share, "col", [(i, i ^ 2) for i in range(8)])
    product, done = accumulate(
        table_p, h_dense, None, [x1], ((4, 1, 1),), ready=early_groups, early=dense
    )
    integrals, terms = finish(atoms)
    dense2 = unpack(table_p, [q2], ((4, -2, 0),))
    q3, integrals, terms, dense2, done = together((q3, integrals, terms, dense2, done))

    q4 = step(front(q3, done))
    x3 = swap(q3)
    product, _ = accumulate(
        table_p, h_dense, product, [x2], ((4, 2, 1),), ready=((4, -2, 0),), early=dense2
    )
    product, _ = accumulate(
        table_p, h_dense, product, [q3, x3], ((4, -3, 0), (4, 3, 1)), local=(terms, dense)
    )
    q4, product = together((q4, product))
    x4 = swap(q4)
    dense4 = unpack(table_p, [q4], ((2, 4, 0),))
    product, _ = accumulate(
        table_p, h_dense, product, [x4], ((2, 4, 1),), ready=((2, 4, 0),), early=dense4
    )
    return (density, integrals, product)


def solution(mesh):
    return jax.shard_map(
        on_device,
        mesh=mesh,
        in_specs=(
            P(("row", "col"), None),
            P(("row", "col")),
            P(("row", "col")),
            P(("row", "col")),
            P("row", "col", None),
            P(),
            P("row", "col"),
            P("row", "col"),
        ),
        out_specs=(P("row", "col", None), P(("row", "col"), None), P("row", "col")),
        check_vma=False,
    )
```
